128 devices in a mesh: az: 32 (over y, x_hi, z), ax: 4 (over x_lo, core).
Axes of the slice: x: 4 (x_hi: 2, x_lo: 2; x = x_hi * 2 + x_lo), y: 4, z: 4, core: 2. Of those that a mesh axis runs over, the one named last changes fastest.
Arguments:
- start_field: float32 [16, 3, 64, 32, 512], P(None, None, 'az', 'ax'), may hold values from -4 to 4
- reluctivity: float32 [3, 64, 32, 512], P(None, 'az', 'ax'), may hold values from 0.05 to 1
- lamination: int32 [64, 32, 512], P('az', 'ax'), may hold values 0 or 1
- magnets: int32 [64, 32, 512], P('az', 'ax'), may hold values 0 or 1
- region_ids: int32 [64, 32, 512], P('az', 'ax'), may hold values from 0 to 127, as said below
- pieces: float32 [3, 16, 128], P(None, None, 'az'), may hold values from -5 to 5
- slot_map: int32 [16, 128], replicated, may hold values from 0 to 127, each once within a row
Outputs:
- solution_field: float32 [16, 3, 64, 32, 512], P(None, None, 'az', 'ax')
- residual: float32 [16, 3, 64, 32, 512], P(None, None, 'az', 'ax')
The draws below stay inside these ranges and needn't reach their ends.
Inputs may be any that keep to these rules, and one draw needn't show every extreme that they name: `region_ids`: a cell of azimuthal sector s, the cells s * 2 to (s + 1) * 2 - 1 along the azimuth, holds a slot from s * 4 to (s + 1) * 4 - 1. `slot_map`: each row is a permutation.
All inputs are finite; a program needn't handle non-finite values. No bound on the sum of `lamination` or of `magnets` on one device may be relied on, other than what follows from the above.
Results may differ from the reference program's by a relative error of at most 0.00002.
Values sent between devices are 32-bit elements; how exact they have to be, the bound alone decides.
No kernel may reach another device: no remote copies, remote signals or barrier semaphores. Data moves between devices by JAX's collectives and lax.ppermute only.
A program may use at most 128 MiB of HBM per device.

```python
import math
import jax
import jax.numpy as jnp
from jax import lax

DEVS = 16
REG_DEV = 4
CA = 2
R = 512
NA = 64
NZ = 32
REGIONS = 128


def draw_region_ids(key, part):
    local = jax.random.randint(key, (NA, NZ, R), 0, REG_DEV)
    sector = (jnp.arange(NA) // CA).astype(jnp.int32)
    return (sector[:, None, None] * REG_DEV + local).astype(jnp.int32)


def touch_ends(values, rng, least, largest):
    longest = values.shape.index(max(values.shape))
    spots = []
    for shift in (0, 1):
        where = [jax.random.randint(jax.random.fold_in(rng, axis), (), 0, length) for axis, length in enumerate(values.shape)]
        where[longest] = (where[longest] + shift) % values.shape[longest]
        spots.append(tuple(where))
    return values.at[spots[0]].set(least).at[spots[1]].set(largest)


def levels(rng, dims, shards, low, largest):
    level = 1.0
    for dim, parts in shards:
        draws = jax.random.uniform(jax.random.fold_in(jax.random.fold_in(rng, 6), dim), (parts,), jnp.float32, low / len(shards), largest / len(shards))
        level = level * jnp.repeat(jnp.exp(draws), dims[dim] // parts).reshape((-1,) + (1,) * (len(dims) - 1 - dim))
    return level


def bell_draw(stream_key, extent, spread, reach, shards=(), kind=jnp.bfloat16):
    values = spread * jax.random.normal(stream_key, extent, jnp.float32)
    if shards:
        values = values * levels(stream_key, extent, shards, -0.22, 0.18)
    return jnp.clip(values, -reach, reach).astype(kind)


def setup_inputs(seed: int = 0) -> dict:
    keys = jax.random.split(jax.random.key(seed), 8)
    return {
        "start_field": bell_draw(keys[0], (DEVS, 3, NA, NZ, R), 0.5, 4.0, ((2, 32), (3, 4)), jnp.float32),
        "reluctivity": jnp.clip(jnp.exp(math.log(1.0) - 2.9957323 * jax.random.uniform(keys[1], (3, NA, NZ, R), jnp.float32) ** levels(keys[1], (3, NA, NZ, R), ((1, 32), (2, 4)), -0.2, 0.2)), 0.05, 1.0),
        "lamination": touch_ends((jax.random.randint(keys[2], (NA, NZ, R), 0, 2) < 1).astype(jnp.int32), jax.random.fold_in(keys[2], 1), 0, 1),
        "magnets": touch_ends((jax.random.randint(keys[3], (NA, NZ, R), 0, 3) < 1).astype(jnp.int32), jax.random.fold_in(keys[3], 1), 0, 1),
        "region_ids": draw_region_ids(jax.random.fold_in(keys[7], 71), 0),
        "pieces": bell_draw(keys[5], (3, DEVS, REGIONS), 1.0, 5.0, ((2, 32),), jnp.float32),
        "slot_map": jax.vmap(lambda own: jax.random.permutation(own, REGIONS))(jax.random.split(keys[6], DEVS)).reshape((DEVS, REGIONS)).astype(jnp.int32),
    }


mass_term = 1.0
cheb_centre = 8.5
cheb_halfwidth = 7.5
cheb_sigma = cheb_centre / cheb_halfwidth
rho_first = 1.0 / cheb_sigma
rho_second = 1.0 / (2.0 * cheb_sigma - rho_first)


def forward_az(values):
    return jnp.roll(values, -1, axis=0) - values


def forward_ax(values):
    return jnp.concatenate([values[:, 1:], jnp.zeros_like(values[:, :1])], axis=1) - values


def forward_radial(values):
    return jnp.concatenate([values[..., 1:], jnp.zeros_like(values[..., :1])], axis=-1) - values


def backward_az(values):
    return values - jnp.roll(values, 1, axis=0)


def backward_ax(values):
    return values - jnp.concatenate([jnp.zeros_like(values[:, :1]), values[:, :-1]], axis=1)


def backward_radial(values):
    return values - jnp.concatenate([jnp.zeros_like(values[..., :1]), values[..., :-1]], axis=-1)


def residual_of(field, reluct, source):
    flux = jnp.stack([
        forward_ax(field[2]) - forward_radial(field[1]),
        forward_radial(field[0]) - forward_az(field[2]),
        forward_az(field[1]) - forward_ax(field[0])], axis=0)
    intensity = reluct * (flux - source)
    curl = jnp.stack([
        backward_ax(intensity[2]) - backward_radial(intensity[1]),
        backward_radial(intensity[0]) - backward_az(intensity[2]),
        backward_az(intensity[1]) - backward_ax(intensity[0])], axis=0)
    return -curl - mass_term * field


def reference(start_field, reluctivity, lamination, magnets, region_ids, pieces, slot_map):
    axial = jnp.array([0.0, 1.0, 0.0], jnp.float32)
    reluct = reluctivity * (1.0 + 3.0 * lamination.astype(jnp.float32)[None] * axial[:, None, None, None])
    magnet_float = magnets.astype(jnp.float32)

    def one_deviation(index):
        table = pieces[:, index]
        slots = slot_map[index][region_ids]
        source = jnp.take(table, slots, axis=1) * magnet_float[None]
        start = start_field[index]
        first_res = residual_of(start, reluct, source)
        first_dir = first_res / cheb_centre
        middle = start + first_dir
        second_res = residual_of(middle, reluct, source)
        second_dir = (rho_second * rho_first) * first_dir + (2.0 * rho_second / cheb_halfwidth) * second_res
        final = middle + second_dir
        return final, residual_of(final, reluct, source)

    solution_field, residual = lax.map(one_deviation, jnp.arange(DEVS, dtype=jnp.int32))
    return (solution_field, residual)
```

```python
import functools

import jax
import jax.numpy as jnp
from jax import lax
from jax.experimental import pallas as pl
from jax.experimental.pallas import tpu as pltpu
from jax.sharding import PartitionSpec as P

mass_term = 1.0
cheb_centre = 8.5
cheb_halfwidth = 7.5
cheb_sigma = cheb_centre / cheb_halfwidth
rho_first = 1.0 / cheb_sigma
rho_second = 1.0 / (2.0 * cheb_sigma - rho_first)

VMEM = pl.BlockSpec(memory_space=pltpu.VMEM)
SMEM = pl.BlockSpec(memory_space=pltpu.SMEM)
PARAMS = pltpu.CompilerParams(vmem_limit_bytes=48 * 1024 * 1024)


def moved(value, shift_az, shift_ax):
    count_az, count_ax = lax.axis_size("az"), lax.axis_size("ax")
    pairs = [
        (a * count_ax + q, (a + shift_az) % count_az * count_ax + q + shift_ax)
        for a in range(count_az)
        for q in range(count_ax)
        if 0 <= q + shift_ax < count_ax
    ]
    return lax.ppermute(value, ("az", "ax"), pairs)


def lanes(shape):
    return lax.broadcasted_iota(jnp.int32, shape, 1)


def rows(shape):
    return lax.broadcasted_iota(jnp.int32, shape, 0)


def radial_next(v):
    n = v.shape[1]
    return jnp.where(lanes(v.shape) == n - 1, 0.0, pltpu.roll(v, n - 1, 1))


def radial_prev(v):
    return jnp.where(lanes(v.shape) == 0, 0.0, pltpu.roll(v, 1, 1))


def axial_next(v, row):
    n = v.shape[0]
    return jnp.where(rows(v.shape) == n - 1, row, pltpu.roll(v, n - 1, 0))


def axial_prev(v, row):
    return jnp.where(rows(v.shape) == 0, row, pltpu.roll(v, 1, 0))


def pack(d, devs, a, minus, plus, ax_minus, ax_plus, corner_a, corner_b):
    top = a[0][0].shape[0] - 1
    minus[2 * d] = a[1][0]
    minus[2 * d + 1] = a[2][0]
    plus[2 * d] = radial_next(a[0][1]) - a[0][1] + a[2][1]
    plus[2 * d + 1] = a[0][1] - axial_next(a[0][1], 0.0) - a[1][1]
    for i in range(2):
        ax_minus[pl.ds(i * devs + d, 1)] = a[0][i][0:1]
        ax_minus[pl.ds((2 + i) * devs + d, 1)] = a[2][i][0:1]
        end = a[1][i][top:]
        ax_plus[pl.ds(i * devs + d, 1)] = end - radial_next(end) - a[2][i][top:]
    ax_plus[pl.ds(2 * devs + d, 1)] = a[1][1][top:] - a[1][0][top:] + a[0][0][top:]
    ax_plus[pl.ds(3 * devs + d, 1)] = a[0][1][top:] - a[1][1][top:]
    corner_a[pl.ds(d, 1)] = a[0][1][0:1]
    corner_b[pl.ds(d, 1)] = a[1][0][top:]


def first_kernel(
    a_ref, reluct_ref, lam_ref, mag_ref, reg_ref, base_ref,
    minus, plus, ax_minus, ax_plus, corner_a, corner_b, nu_ref, code_ref,
):
    devs = a_ref.shape[0]
    last = a_ref.shape[3] - 1
    base = base_ref[0]
    for i in range(2):
        axial = 1.0 + 3.0 * lam_ref[i].astype(jnp.float32)
        nu_ref[0, i] = reluct_ref[0, i]
        nu_ref[1, i] = reluct_ref[1, i] * axial
        nu_ref[2, i] = reluct_ref[2, i]
        code_ref[i] = jnp.where(mag_ref[i] == 1, reg_ref[i] - base + 1, 0).astype(jnp.float32)
    plus[2 * devs] = nu_ref[1, 1]
    plus[2 * devs + 1] = nu_ref[2, 1]
    plus[2 * devs + 2] = code_ref[1]
    for i in range(2):
        ax_plus[pl.ds(4 * devs + i, 1)] = nu_ref[0, i, last:]
        ax_plus[pl.ds(4 * devs + 2 + i, 1)] = nu_ref[2, i, last:]
        ax_plus[pl.ds(4 * devs + 4 + i, 1)] = code_ref[i, last:]
        ax_plus[pl.ds(4 * devs + 6 + i, 1)] = jnp.zeros_like(code_ref[i, last:])

    @pl.loop(0, devs)
    def _(d):
        a = [[a_ref[d, c, i] for i in range(2)] for c in range(3)]
        pack(d, devs, a, minus, plus, ax_minus, ax_plus, corner_a, corner_b)


def picked(code, values):
    out = jnp.zeros_like(code)
    for k, value in enumerate(values):
        out = jnp.where(code == k + 1.0, value, out)
    return out


def source_kernel(
    table_ref, slots_ref, where_ref, nu_ref, code_ref, halo_ref, ax_halo_ref,
    src_ref, src_az_ref, src_ax_ref,
):
    devs = src_ref.shape[0]
    here, behind, per = where_ref[0], where_ref[1], where_ref[2]
    count = table_ref.shape[1] // (3 * devs)

    @pl.loop(0, devs)
    def _(d):
        def value(c, first, k):
            slot = slots_ref[d, first + k]
            return table_ref[slot // count, (c * devs + d) * count + slot % count]

        for c in range(3):
            own = [value(c, here, k) for k in range(count)]
            for i in range(2):
                src_ref[d, c, i] = nu_ref[c, i] * picked(code_ref[i], own)
                if c != 1:
                    at = (c + i) * devs
                    src_ax_ref[pl.ds(at + d, 1)] = ax_halo_ref[pl.ds(4 * devs + c + i, 1)] * picked(
                        ax_halo_ref[pl.ds(4 * devs + 4 + i, 1)], own
                    )
            if c != 0:
                before = [value(c, behind, k) for k in range(count)]
                src_az_ref[2 * d + c - 1] = halo_ref[2 * devs + c - 1] * picked(halo_ref[2 * devs + 2], before)


def step_kernel(
    stage, a_ref, start_ref, nu_ref, src_ref, nu_az_ref, src_az_ref, nu_ax_ref, src_ax_ref,
    ahead, behind, ax_ahead, ax_behind, mine, corner_c, corner_d, out_ref, *rest,
):
    devs = a_ref.shape[0]
    *packed, edge = rest
    nu_az = 2 * devs
    for at, own, sign in ((0, 2, 1.0), (1, 3, 1.0), (2, 0, -1.0), (3, 1, -1.0)):
        part = pl.ds(at * devs, devs)
        flux = ax_behind[part] + sign * mine[pl.ds(own * devs, devs)]
        if at == 3:
            flux = flux + corner_d[...]
        edge[part] = nu_ax_ref[pl.ds(4 * devs + at, 1)] * flux - src_ax_ref[part]

    @pl.loop(0, devs)
    def _(d):
        a = [[a_ref[d, c, i] for i in range(2)] for c in range(3)]
        up = [None, ahead[2 * d], ahead[2 * d + 1]]
        inten = [[None, None], [None, None], [None, None]]
        for i in range(2):
            next1 = a[1][1] if i == 0 else up[1]
            next2 = a[2][1] if i == 0 else up[2]
            row0 = ax_ahead[pl.ds(i * devs + d, 1)]
            row2 = ax_ahead[pl.ds((2 + i) * devs + d, 1)]
            flux = (
                (axial_next(a[2][i], row2) - a[2][i]) - (radial_next(a[1][i]) - a[1][i]),
                (radial_next(a[0][i]) - a[0][i]) - (next2 - a[2][i]),
                (next1 - a[1][i]) - (axial_next(a[0][i], row0) - a[0][i]),
            )
            for c in range(3):
                inten[c][i] = nu_ref[c, i] * flux[c] - src_ref[d, c, i]
        corner = jnp.where(rows(a[1][0].shape) == a[1][0].shape[0] - 1, corner_c[pl.ds(d, 1)], 0.0)
        back1 = nu_az_ref[nu_az] * (behind[2 * d] - a[2][0]) - src_az_ref[2 * d]
        back2 = nu_az_ref[nu_az + 1] * (behind[2 * d + 1] + a[1][0] - corner) - src_az_ref[2 * d + 1]
        new = [[None, None], [None, None], [None, None]]
        for i in range(2):
            prev1 = back1 if i == 0 else inten[1][0]
            prev2 = back2 if i == 0 else inten[2][0]
            row0 = edge[pl.ds(i * devs + d, 1)]
            row2 = edge[pl.ds((2 + i) * devs + d, 1)]
            i0, i1, i2 = inten[0][i], inten[1][i], inten[2][i]
            curl = (
                (i2 - axial_prev(i2, row2)) - (i1 - radial_prev(i1)),
                (i0 - radial_prev(i0)) - (i2 - prev2),
                (i1 - prev1) - (i0 - axial_prev(i0, row0)),
            )
            for c in range(3):
                res = -curl[c] - mass_term * a[c][i]
                if stage == 0:
                    value = a[c][i] + res * (1.0 / cheb_centre)
                elif stage == 1:
                    first_dir = a[c][i] - start_ref[d, c, i]
                    value = a[c][i] + (
                        rho_second * rho_first * first_dir + 2.0 * rho_second / cheb_halfwidth * res
                    )
                else:
                    value = res
                out_ref[d, c, i] = value
                new[c][i] = value
        if stage < 2:
            pack(d, devs, new, *packed)


def f32(*shape):
    return jax.ShapeDtypeStruct(shape, jnp.float32)


def shards(start_field, reluctivity, lamination, magnets, region_ids, pieces, slot_map):
    devs, comps, cells_az, cells_ax, radial = start_field.shape
    count_az = lax.axis_size("az")
    per = pieces.shape[2]
    me = lax.axis_index("az")
    here = me * per
    behind_slots = (me + count_az - 1) % count_az * per
    where = jnp.stack([here, behind_slots, jnp.int32(per)]).astype(jnp.int32)

    messages = [
        f32(2 * devs, cells_ax, radial),
        f32(2 * devs, cells_ax, radial),
        f32(4 * devs, radial),
        f32(4 * devs, radial),
        f32(devs, radial),
        f32(devs, radial),
    ]
    first = list(messages)
    first[1] = f32(2 * devs + 3, cells_ax, radial)
    first[3] = f32(4 * devs + 8, radial)
    *packed, nu, code = pl.pallas_call(
        first_kernel,
        out_shape=first + [f32(*reluctivity.shape), f32(*lamination.shape)],
        in_specs=[VMEM] * 5 + [SMEM],
        out_specs=[VMEM] * 8,
        compiler_params=PARAMS,
    )(start_field, reluctivity, lamination, magnets, region_ids, where)

    def exchange(minus, plus, ax_minus, ax_plus, corner_a, corner_b):
        return (
            moved(minus, -1, 0),
            moved(plus, 1, 0),
            moved(ax_minus, 0, -1),
            moved(ax_plus, 0, 1),
            moved(corner_a, 1, -1),
            moved(corner_b, -1, 1),
        )

    halos = exchange(*packed)
    flat = pieces.reshape(1, comps * devs * per)
    table = lax.all_to_all(
        jnp.broadcast_to(flat, (count_az, comps * devs * per)), "az", 0, 0, tiled=True
    )
    nu_az, nu_ax = halos[1], halos[3]
    src, src_az, src_ax = pl.pallas_call(
        source_kernel,
        out_shape=[f32(*start_field.shape), f32(2 * devs, cells_ax, radial), f32(4 * devs, radial)],
        in_specs=[SMEM] * 3 + [VMEM] * 4,
        out_specs=[VMEM] * 3,
        compiler_params=PARAMS,
    )(table, slot_map, where, nu, code, nu_az, nu_ax)

    field, outs = start_field, []
    for stage in range(3):
        ahead, behind, ax_ahead, ax_behind, corner_c, corner_d = halos
        field, *new_packed = pl.pallas_call(
            functools.partial(step_kernel, stage),
            out_shape=[f32(*start_field.shape)] + (messages if stage < 2 else []),
            in_specs=[VMEM] * 15,
            out_specs=[VMEM] * (7 if stage < 2 else 1),
            scratch_shapes=[pltpu.VMEM((4 * devs, radial), jnp.float32)],
            compiler_params=PARAMS,
        )(
            field, start_field, nu, src, nu_az, src_az, nu_ax, src_ax,
            ahead, behind, ax_ahead, ax_behind, packed[2], corner_c, corner_d,
        )
        outs.append(field)
        if stage < 2:
            packed = new_packed
            halos = exchange(*packed)
    return outs[1], outs[2]


def solution(mesh):
    placed = (
        P(None, None, "az", "ax", None),
        P(None, "az", "ax", None),
        P("az", "ax", None),
        P("az", "ax", None),
        P("az", "ax", None),
        P(None, None, "az"),
        P(),
    )
    return jax.shard_map(
        shards,
        mesh=mesh,
        in_specs=placed,
        out_specs=(P(None, None, "az", "ax", None), P(None, None, "az", "ax", None)),
        check_vma=False,
    )
```

```python
import functools

import jax
import jax.numpy as jnp
from jax import lax
from jax.experimental import pallas as pl
from jax.experimental.pallas import tpu as pltpu
from jax.sharding import PartitionSpec as P

mass_term = 1.0
cheb_centre = 8.5
cheb_halfwidth = 7.5
cheb_sigma = cheb_centre / cheb_halfwidth
rho_first = 1.0 / cheb_sigma
rho_second = 1.0 / (2.0 * cheb_sigma - rho_first)

mix_second = rho_second * rho_first
step_second = 2.0 * rho_second / cheb_halfwidth

VMEM = pl.BlockSpec(memory_space=pltpu.VMEM)
SMEM = pl.BlockSpec(memory_space=pltpu.SMEM)
HBM = pl.BlockSpec(memory_space=pltpu.HBM)
MIB = 1024 * 1024
LIMIT = 16 * MIB
LIMIT_FIRST = 63 * MIB


def moved(value, shift_az, shift_ax):
    count_az, count_ax = lax.axis_size("az"), lax.axis_size("ax")
    pairs = [
        (a * count_ax + q, (a + shift_az) % count_az * count_ax + q + shift_ax)
        for a in range(count_az)
        for q in range(count_ax)
        if 0 <= q + shift_ax < count_ax
    ]
    return lax.ppermute(value, ("az", "ax"), pairs)


def lanes(shape):
    return lax.broadcasted_iota(jnp.int32, shape, 1)


def rows(shape):
    return lax.broadcasted_iota(jnp.int32, shape, 0)


def radial_next(v):
    tile = 128
    rolled = [pltpu.roll(v[:, at : at + tile], tile - 1, 1) for at in range(0, v.shape[1], tile)]
    last = lanes(rolled[0].shape) == tile - 1
    rolled.append(jnp.zeros_like(rolled[0]))
    return jnp.concatenate(
        [jnp.where(last, later, part) for part, later in zip(rolled, rolled[1:])], axis=1
    )


def radial_prev(v):
    tile = 128
    rolled = [pltpu.roll(v[:, at : at + tile], 1, 1) for at in range(0, v.shape[1], tile)]
    first = lanes(rolled[0].shape) == 0
    rolled.insert(0, jnp.zeros_like(rolled[0]))
    return jnp.concatenate(
        [jnp.where(first, sooner, part) for sooner, part in zip(rolled, rolled[1:])], axis=1
    )


def axial_next(v, row):
    n = v.shape[0]
    return jnp.where(rows(v.shape) == n - 1, row, pltpu.roll(v, n - 1, 0))


def axial_prev(v, row):
    return jnp.where(rows(v.shape) == 0, row, pltpu.roll(v, 1, 0))


def block(k, height):
    return pl.ds(pl.multiple_of(k * height, height), height)


def pack_az(d, height, a, minus, plus):
    minus[block(2 * d, height)] = a[1][0]
    minus[block(2 * d + 1, height)] = a[2][0]
    plus[block(2 * d, height)] = radial_next(a[0][1]) - a[0][1] + a[2][1]
    plus[block(2 * d + 1, height)] = a[0][1] - axial_next(a[0][1], 0.0) - a[1][1]


def pack_ax(d, devs, a, ax_minus, ax_plus):
    top = a[0][0].shape[0] - 1
    for i in range(2):
        ax_minus[pl.ds(i * devs + d, 1)] = a[0][i][0:1]
        ax_minus[pl.ds((2 + i) * devs + d, 1)] = a[2][i][0:1]
        end = a[1][i][top:]
        ax_plus[pl.ds(i * devs + d, 1)] = end - radial_next(end) - a[2][i][top:]
    ax_plus[pl.ds(2 * devs + d, 1)] = a[1][1][top:] - a[1][0][top:] + a[0][0][top:]
    ax_plus[pl.ds(3 * devs + d, 1)] = a[0][1][top:] - a[1][1][top:]


def edge_kernel(
    per, a_hbm, reluct_hbm, lam_hbm, mag_hbm, reg_hbm, slots_hbm,
    ax_minus, ax_plus, nu_ref, code_ref, offset_ref,
    a_ref, lam_ref, mag_ref, reg_ref, slots_ref, sems,
):
    devs = a_ref.shape[0]
    top = a_ref.shape[3] - 1
    parts = 2
    some = devs // parts
    copies = [
        pltpu.make_async_copy(reluct_hbm, nu_ref, sems.at[0]),
        pltpu.make_async_copy(lam_hbm, lam_ref, sems.at[1]),
        pltpu.make_async_copy(mag_hbm, mag_ref, sems.at[2]),
        pltpu.make_async_copy(reg_hbm, reg_ref, sems.at[3]),
        pltpu.make_async_copy(slots_hbm, slots_ref, sems.at[4]),
    ]
    for part in range(parts):
        at = pl.ds(part * some, some)
        copies.append(pltpu.make_async_copy(a_hbm.at[at], a_ref.at[at], sems.at[5 + part]))
    for copy in copies:
        copy.start()
    for copy in copies[:5]:
        copy.wait()

    base = lax.axis_index("az") * per
    slots = slots_ref[...]
    count = slots.shape[1]
    slots = pltpu.roll(slots, lax.rem(2 * count - base + per, count), 1)
    row = lax.div(slots, jnp.int32(per))
    offset_ref[...] = row * (3 * devs * per) + (slots - row * per)
    for i in range(2):
        nu_ref[1, i] = nu_ref[1, i] * (1.0 + 3.0 * lam_ref[i].astype(jnp.float32))
        code_ref[i] = jnp.where(mag_ref[i] == 1, reg_ref[i] - base + 1, 0).astype(jnp.float32)
    for i in range(2):
        at = 5 * devs + i
        ax_plus[pl.ds(at, 1)] = nu_ref[0, i, top:]
        ax_plus[pl.ds(at + 2, 1)] = nu_ref[2, i, top:]
        ax_plus[pl.ds(at + 4, 1)] = code_ref[i, top:]
        ax_plus[pl.ds(at + 6, 1)] = jnp.zeros_like(code_ref[i, top:])

    for part in range(parts):
        copies[5 + part].wait()

        @pl.loop(part * some, (part + 1) * some)
        def _(d):
            a = [[a_ref[d, c, i] for i in range(2)] for c in range(3)]
            pack_ax(d, devs, a, ax_minus, ax_plus)
            ax_plus[pl.ds(4 * devs + d, 1)] = a[1][0][top:]


def plane_kernel(a_ref, nu_ref, code_ref, ax_ahead, ax_behind, minus, plus):
    devs, height = a_ref.shape[0], a_ref.shape[3]
    end = 2 * devs * height
    minus[pl.ds(end, devs)] = ax_behind[pl.ds(4 * devs, devs)]
    plus[pl.ds(end, devs)] = ax_ahead[pl.ds(devs, devs)]
    plus[pl.ds(end + devs, height)] = nu_ref[1, 1]
    plus[pl.ds(end + devs + height, height)] = nu_ref[2, 1]
    plus[pl.ds(end + devs + 2 * height, height)] = code_ref[1]

    @pl.loop(0, devs)
    def _(d):
        a = [[a_ref[d, c, i] for i in range(2)] for c in range(3)]
        pack_az(d, height, a, minus, plus)


def picked(code, values):
    out = jnp.zeros_like(code)
    for k, value in enumerate(values):
        out = jnp.where(code == k + 1.0, value, out)
    return out


def advanced(stage, value, start, curl):
    if stage == 0:
        return value * (1.0 - mass_term / cheb_centre) - curl * (1.0 / cheb_centre)
    if stage == 1:
        return (
            value * (1.0 + mix_second - mass_term * step_second) - start * mix_second - curl * step_second
        )
    return -curl - mass_term * value


def step_kernel(stage, per, *refs):
    it = iter(refs)
    a_ref, nu_ref, nu_az_ref, nu_ax_ref = next(it), next(it), next(it), next(it)
    ahead, behind, ax_ahead, ax_behind, mine = [next(it) for _ in range(5)]
    if stage == 0:
        code_ref, offset_ref, table_ref = next(it), next(it), next(it)
    else:
        src_ref, src_az_ref, src_ax_ref, track0 = [next(it) for _ in range(4)]
    track = track0 if stage == 1 else None
    if stage == 1:
        start_ref = next(it)
    if stage == 2:
        track = next(it)
    out_ref = next(it)
    if stage < 2:
        minus, plus, ax_minus, ax_plus, next_track = [next(it) for _ in range(5)]
    if stage == 0:
        src_ref, src_az_ref, src_ax_ref = next(it), next(it), next(it)
    edge, corner = next(it), next(it)
    devs, height = a_ref.shape[0], a_ref.shape[3]
    top = height - 1
    end = 2 * devs * height
    nu_az = end + devs
    nu_ax = 5 * devs
    every = pl.ds(0, devs)
    after = pl.ds(devs, devs)

    if stage == 0:
        corner[every] = behind[pl.ds(end, devs)]
        corner[after] = ahead[pl.ds(end, devs)]
    else:
        curl = ax_ahead[pl.ds(4 * devs, devs)] - track[pl.ds(2 * devs, devs)]
        value = advanced(stage - 1, track[every], track0[every], curl)
        open_end = lax.axis_index("ax") == lax.axis_size("ax") - 1
        corner[every] = jnp.where(open_end, 0.0, value)
        curl = ahead[pl.ds(end, devs)] + track[pl.ds(3 * devs, devs)]
        corner[after] = advanced(stage - 1, track[after], track0[after], curl)

    def values(d, c, first):
        return [
            table_ref[offset_ref[d, first + k] + (c * devs + d) * per] for k in range(per)
        ]

    if stage == 0:

        @pl.loop(0, devs)
        def _(d):
            for c in (0, 2):
                own = values(d, c, per)
                for i in range(2):
                    src_ax_ref[pl.ds((c + i) * devs + d, 1)] = nu_ax_ref[pl.ds(nu_ax + c + i, 1)] * picked(
                        nu_ax_ref[pl.ds(nu_ax + 4 + i, 1)], own
                    )

    for at, own, sign in ((0, 2, 1.0), (1, 3, 1.0), (2, 0, -1.0), (3, 1, -1.0)):
        part = pl.ds(at * devs, devs)
        flux = ax_behind[part] + sign * mine[pl.ds(own * devs, devs)]
        if at == 3:
            flux = flux + corner[after]
        edge[part] = nu_ax_ref[pl.ds(nu_ax + at, 1)] * flux - src_ax_ref[part]
    if stage < 2:
        before = edge[every]
        minus[pl.ds(end, devs)] = before - radial_prev(before) - edge[pl.ds(2 * devs, devs)]
        next_track[pl.ds(0, 2 * devs)] = corner[...]
        next_track[pl.ds(3 * devs, devs)] = edge[pl.ds(3 * devs, devs)]

    @pl.loop(0, devs)
    def _(d):
        a = [[a_ref[d, c, i] for i in range(2)] for c in range(3)]
        up = [None, ahead[block(2 * d, height)], ahead[block(2 * d + 1, height)]]
        inten = [[None, None], [None, None], [None, None]]
        own = [values(d, c, per) for c in range(3)] if stage == 0 else None
        for i in range(2):
            next1 = a[1][1] if i == 0 else up[1]
            next2 = a[2][1] if i == 0 else up[2]
            row0 = ax_ahead[pl.ds(i * devs + d, 1)]
            row2 = ax_ahead[pl.ds((2 + i) * devs + d, 1)]
            flux = (
                (axial_next(a[2][i], row2) - a[2][i]) - (radial_next(a[1][i]) - a[1][i]),
                (radial_next(a[0][i]) - a[0][i]) - (next2 - a[2][i]),
                (next1 - a[1][i]) - (axial_next(a[0][i], row0) - a[0][i]),
            )
            for c in range(3):
                if stage == 0:
                    src = nu_ref[c, i] * picked(code_ref[i], own[c])
                    src_ref[d, c, i] = src
                else:
                    src = src_ref[d, c, i]
                inten[c][i] = nu_ref[c, i] * flux[c] - src
        back_src = [None, None]
        for c in range(1, 3):
            if stage == 0:
                src = nu_az_ref[block(2 * devs + 1 + c, height)] * picked(
                    nu_az_ref[pl.ds(nu_az + 2 * height, height)], values(d, c, 0)
                )
                src_az_ref[2 * d + c - 1] = src
            else:
                src = src_az_ref[2 * d + c - 1]
            back_src[c - 1] = src
        beyond = jnp.where(rows(a[1][0].shape) == top, corner[pl.ds(d, 1)], 0.0)
        back1 = nu_az_ref[pl.ds(nu_az, height)] * (behind[block(2 * d, height)] - a[2][0]) - back_src[0]
        back2 = (
            nu_az_ref[pl.ds(nu_az + height, height)]
            * (behind[block(2 * d + 1, height)] + a[1][0] - beyond)
            - back_src[1]
        )
        new = [[None, None], [None, None], [None, None]]
        for i in range(2):
            prev1 = back1 if i == 0 else inten[1][0]
            prev2 = back2 if i == 0 else inten[2][0]
            row0 = edge[pl.ds(i * devs + d, 1)]
            row2 = edge[pl.ds((2 + i) * devs + d, 1)]
            i0, i1, i2 = inten[0][i], inten[1][i], inten[2][i]
            curl = (
                (i2 - axial_prev(i2, row2)) - (i1 - radial_prev(i1)),
                (i0 - radial_prev(i0)) - (i2 - prev2),
                (i1 - prev1) - (i0 - axial_prev(i0, row0)),
            )
            for c in range(3):
                start = start_ref[d, c, i] if stage == 1 else None
                value = advanced(stage, a[c][i], start, curl[c])
                out_ref[d, c, i] = value
                new[c][i] = value
        if stage < 2:
            first1, first2 = back1[0:1], back2[0:1]
            ax_minus[pl.ds(4 * devs + d, 1)] = first2 - (first1 - radial_prev(first1))
            next_track[pl.ds(2 * devs + d, 1)] = back2[top:]
            pack_az(d, height, new, minus, plus)
            pack_ax(d, devs, new, ax_minus, ax_plus)


def f32(*shape):
    return jax.ShapeDtypeStruct(shape, jnp.float32)


def shards(start_field, reluctivity, lamination, magnets, region_ids, pieces, slot_map):
    devs, comps, cells_az, cells_ax, radial = start_field.shape
    count_az = lax.axis_size("az")
    per = pieces.shape[2]
    whole = 2 * devs * cells_ax

    field_like = f32(*start_field.shape)
    edges = [
        f32(4 * devs, radial),
        f32(5 * devs + 8, radial),
        f32(*reluctivity.shape),
        f32(*lamination.shape),
        jax.ShapeDtypeStruct(slot_map.shape, jnp.int32),
    ]
    ax_minus, ax_plus, nu, code, offset = pl.pallas_call(
        functools.partial(edge_kernel, per),
        out_shape=edges,
        in_specs=[HBM] * 6,
        out_specs=[VMEM] * len(edges),
        scratch_shapes=[pltpu.VMEM(start_field.shape, jnp.float32)]
        + [pltpu.VMEM(lamination.shape, jnp.int32)] * 3
        + [pltpu.VMEM(slot_map.shape, jnp.int32), pltpu.SemaphoreType.DMA((7,))],
        compiler_params=pltpu.CompilerParams(vmem_limit_bytes=LIMIT_FIRST),
    )(start_field, reluctivity, lamination, magnets, region_ids, slot_map)
    ax_ahead, ax_behind = moved(ax_minus, 0, -1), moved(ax_plus, 0, 1)
    planes = [f32(whole + devs, radial), f32(whole + devs + 3 * cells_ax, radial)]
    minus, plus = pl.pallas_call(
        plane_kernel,
        out_shape=planes,
        in_specs=[VMEM] * 5,
        out_specs=[VMEM] * 2,
        compiler_params=pltpu.CompilerParams(vmem_limit_bytes=LIMIT),
    )(start_field, nu, code, ax_ahead, ax_behind)
    halos = (moved(minus, -1, 0), moved(plus, 1, 0), ax_ahead, ax_behind, ax_minus)
    flat = pieces.reshape(1, comps * devs * per)
    table = lax.all_to_all(
        jnp.broadcast_to(flat, (count_az, comps * devs * per)), "az", 0, 0, tiled=True
    ).reshape(-1)
    nu_az, nu_ax = halos[1], halos[3]

    def exchange(minus, plus, ax_minus, ax_plus):
        ahead, behind = moved(minus, -1, 0), moved(plus, 1, 0)
        return ahead, behind, moved(ax_minus, 0, -1), moved(ax_plus, 0, 1), ax_minus

    def step(stage, field, halos, more, more_specs):
        outs = [field_like]
        if stage < 2:
            outs += [
                f32(whole + devs, radial),
                f32(whole, radial),
                f32(5 * devs, radial),
                f32(4 * devs, radial),
                f32(4 * devs, radial),
            ]
        if stage == 0:
            outs += [field_like, f32(2 * devs, cells_ax, radial), f32(4 * devs, radial)]
        return pl.pallas_call(
            functools.partial(step_kernel, stage, per),
            out_shape=outs,
            in_specs=[VMEM] * 9 + more_specs,
            out_specs=[VMEM] * len(outs),
            scratch_shapes=[
                pltpu.VMEM((4 * devs, radial), jnp.float32),
                pltpu.VMEM((2 * devs, radial), jnp.float32),
            ],
            compiler_params=pltpu.CompilerParams(vmem_limit_bytes=LIMIT),
        )(field, nu, nu_az, nu_ax, *halos, *more)

    middle, *rest = step(0, start_field, halos, [code, offset, table], [VMEM, SMEM, SMEM])
    packed, track0, src = rest[:4], rest[4], rest[5:]
    final, *rest = step(1, middle, exchange(*packed), [*src, track0, start_field], [VMEM] * 5)
    packed, track1 = rest[:4], rest[4]
    (residual,) = step(2, final, exchange(*packed), [*src, track0, track1], [VMEM] * 5)
    return final, residual


def solution(mesh):
    placed = (
        P(None, None, "az", "ax", None),
        P(None, "az", "ax", None),
        P("az", "ax", None),
        P("az", "ax", None),
        P("az", "ax", None),
        P(None, None, "az"),
        P(),
    )
    return jax.shard_map(
        shards,
        mesh=mesh,
        in_specs=placed,
        out_specs=(P(None, None, "az", "ax", None), P(None, None, "az", "ax", None)),
        check_vma=False,
    )
```

```python
import functools

import jax
import jax.numpy as jnp
from jax import lax
from jax.experimental import pallas as pl
from jax.experimental.pallas import tpu as pltpu
from jax.sharding import PartitionSpec as P

mass_term = 1.0
cheb_centre = 8.5
cheb_halfwidth = 7.5
cheb_sigma = cheb_centre / cheb_halfwidth
rho_first = 1.0 / cheb_sigma
rho_second = 1.0 / (2.0 * cheb_sigma - rho_first)

mix_second = rho_second * rho_first
step_second = 2.0 * rho_second / cheb_halfwidth

VMEM = pl.BlockSpec(memory_space=pltpu.VMEM)
SMEM = pl.BlockSpec(memory_space=pltpu.SMEM)
HBM = pl.BlockSpec(memory_space=pltpu.HBM)
ANY = pl.BlockSpec(memory_space=pl.ANY)
MIB = 1024 * 1024
LIMIT = 16 * MIB
UNROLL = 4
LIMIT_FIRST = 63 * MIB


def moved(value, shift_az, shift_ax):
    count_az, count_ax = lax.axis_size("az"), lax.axis_size("ax")
    pairs = [
        (a * count_ax + q, (a + shift_az) % count_az * count_ax + q + shift_ax)
        for a in range(count_az)
        for q in range(count_ax)
        if 0 <= q + shift_ax < count_ax
    ]
    return lax.ppermute(value, ("az", "ax"), pairs)


def lanes(shape):
    return lax.broadcasted_iota(jnp.int32, shape, 1)


def rows(shape):
    return lax.broadcasted_iota(jnp.int32, shape, 0)


def radial_next(v):
    tile = 128
    rolled = [pltpu.roll(v[:, at : at + tile], tile - 1, 1) for at in range(0, v.shape[1], tile)]
    last = lanes(rolled[0].shape) == tile - 1
    rolled.append(jnp.zeros_like(rolled[0]))
    return jnp.concatenate(
        [jnp.where(last, later, part) for part, later in zip(rolled, rolled[1:])], axis=1
    )


def radial_prev(v):
    tile = 128
    rolled = [pltpu.roll(v[:, at : at + tile], 1, 1) for at in range(0, v.shape[1], tile)]
    first = lanes(rolled[0].shape) == 0
    rolled.insert(0, jnp.zeros_like(rolled[0]))
    return jnp.concatenate(
        [jnp.where(first, sooner, part) for sooner, part in zip(rolled, rolled[1:])], axis=1
    )


def axial_next(v, row):
    n = v.shape[0]
    return jnp.where(rows(v.shape) == n - 1, row, pltpu.roll(v, n - 1, 0))


def axial_prev(v, row):
    return jnp.where(rows(v.shape) == 0, row, pltpu.roll(v, 1, 0))


def block(k, height):
    return pl.ds(pl.multiple_of(k * height, height), height)


def pack_az(d, height, a, minus, plus):
    minus[block(2 * d, height)] = a[1][0]
    minus[block(2 * d + 1, height)] = a[2][0]
    plus[block(2 * d, height)] = radial_next(a[0][1]) - a[0][1] + a[2][1]
    plus[block(2 * d + 1, height)] = a[0][1] - axial_next(a[0][1], 0.0) - a[1][1]


def pack_ax(d, devs, a, ax_minus, ax_plus):
    top = a[0][0].shape[0] - 1
    for i in range(2):
        ax_minus[pl.ds(i * devs + d, 1)] = a[0][i][0:1]
        ax_minus[pl.ds((2 + i) * devs + d, 1)] = a[2][i][0:1]
        end = a[1][i][top:]
        ax_plus[pl.ds(i * devs + d, 1)] = end - radial_next(end) - a[2][i][top:]
    ax_plus[pl.ds(2 * devs + d, 1)] = a[1][1][top:] - a[1][0][top:] + a[0][0][top:]
    ax_plus[pl.ds(3 * devs + d, 1)] = a[0][1][top:] - a[1][1][top:]


def edge_kernel(
    per, a_hbm, reluct_hbm, lam_hbm, mag_hbm, reg_hbm, slots_hbm,
    ax_minus, ax_plus, nu_ref, code_ref, offset_ref,
    a_ref, lam_ref, mag_ref, reg_ref, slots_ref, sems,
):
    devs = a_ref.shape[0]
    top = a_ref.shape[3] - 1
    parts = 2
    some = devs // parts
    copies = [
        pltpu.make_async_copy(reluct_hbm, nu_ref, sems.at[0]),
        pltpu.make_async_copy(lam_hbm, lam_ref, sems.at[1]),
        pltpu.make_async_copy(mag_hbm, mag_ref, sems.at[2]),
        pltpu.make_async_copy(reg_hbm, reg_ref, sems.at[3]),
        pltpu.make_async_copy(slots_hbm, slots_ref, sems.at[4]),
    ]
    for part in range(parts):
        at = pl.ds(part * some, some)
        copies.append(pltpu.make_async_copy(a_hbm.at[at], a_ref.at[at], sems.at[5 + part]))
    for copy in copies:
        copy.start()
    for copy in copies[:5]:
        copy.wait()

    base = lax.axis_index("az") * per
    slots = slots_ref[...]
    count = slots.shape[1]
    slots = pltpu.roll(slots, lax.rem(2 * count - base + per, count), 1)
    row = lax.div(slots, jnp.int32(per))
    offset_ref[...] = row * (3 * devs * per) + (slots - row * per)
    for i in range(2):
        nu_ref[1, i] = nu_ref[1, i] * (1.0 + 3.0 * lam_ref[i].astype(jnp.float32))
        code_ref[i] = jnp.where(mag_ref[i] == 1, reg_ref[i] - base + 1, 0).astype(jnp.float32)
    for i in range(2):
        at = 5 * devs + i
        ax_plus[pl.ds(at, 1)] = nu_ref[0, i, top:]
        ax_plus[pl.ds(at + 2, 1)] = nu_ref[2, i, top:]
        ax_plus[pl.ds(at + 4, 1)] = code_ref[i, top:]
        ax_plus[pl.ds(at + 6, 1)] = jnp.zeros_like(code_ref[i, top:])

    for part in range(parts):
        copies[5 + part].wait()

        @pl.loop(part * some, (part + 1) * some, unroll=UNROLL)
        def _(d):
            a = [[a_ref[d, c, i] for i in range(2)] for c in range(3)]
            pack_ax(d, devs, a, ax_minus, ax_plus)
            ax_plus[pl.ds(4 * devs + d, 1)] = a[1][0][top:]


def plane_kernel(a_ref, nu_ref, code_ref, minus, plus):
    devs, height = a_ref.shape[0], a_ref.shape[3]
    end = 2 * devs * height + devs
    plus[pl.ds(end, height)] = nu_ref[1, 1]
    plus[pl.ds(end + height, height)] = nu_ref[2, 1]
    plus[pl.ds(end + 2 * height, height)] = code_ref[1]

    @pl.loop(0, devs, unroll=UNROLL)
    def _(d):
        a = [[a_ref[d, c, i] for i in range(2)] for c in range(3)]
        pack_az(d, height, a, minus, plus)


def corner_kernel(devs, ax_ahead, ax_behind, minus_in, plus_in, minus, plus, sems):
    at = pl.ds(2 * devs * (minus.shape[0] // (2 * devs + 2)), devs)
    copies = [
        pltpu.make_async_copy(ax_behind.at[pl.ds(4 * devs, devs)], minus.at[at], sems.at[0]),
        pltpu.make_async_copy(ax_ahead.at[pl.ds(devs, devs)], plus.at[at], sems.at[1]),
    ]
    for copy in copies:
        copy.start()
    for copy in copies:
        copy.wait()


def picked(code, values):
    out = jnp.zeros_like(code)
    for k, value in enumerate(values):
        out = jnp.where(code == k + 1.0, value, out)
    return out


def advanced(stage, value, start, curl):
    if stage == 0:
        return value * (1.0 - mass_term / cheb_centre) - curl * (1.0 / cheb_centre)
    if stage == 1:
        return (
            value * (1.0 + mix_second - mass_term * step_second) - start * mix_second - curl * step_second
        )
    return -curl - mass_term * value


def step_kernel(stage, per, *refs):
    it = iter(refs)
    a_ref, nu_ref, nu_az_ref, nu_ax_ref = next(it), next(it), next(it), next(it)
    ahead, behind, ax_ahead, ax_behind, mine = [next(it) for _ in range(5)]
    if stage == 0:
        code_ref, offset_ref, table_ref = next(it), next(it), next(it)
    else:
        src_ref, src_az_ref, src_ax_ref, track0 = [next(it) for _ in range(4)]
    track = track0 if stage == 1 else None
    if stage == 1:
        start_ref = next(it)
    if stage == 2:
        track = next(it)
    out_ref = next(it)
    if stage < 2:
        minus, plus, ax_minus, ax_plus, next_track = [next(it) for _ in range(5)]
    if stage == 0:
        src_ref, src_az_ref, src_ax_ref = next(it), next(it), next(it)
    if stage == 2:
        final_hbm = next(it)
    edge, corner = next(it), next(it)
    if stage == 2:
        leave = pltpu.make_async_copy(a_ref, final_hbm, next(it))
        leave.start()
    devs, height = a_ref.shape[0], a_ref.shape[3]
    top = height - 1
    end = 2 * devs * height
    nu_az = end + devs
    nu_ax = 5 * devs
    every = pl.ds(0, devs)
    after = pl.ds(devs, devs)

    if stage == 0:
        corner[every] = behind[pl.ds(end, devs)]
        corner[after] = ahead[pl.ds(end, devs)]
    else:
        curl = ax_ahead[pl.ds(4 * devs, devs)] - track[pl.ds(2 * devs, devs)]
        value = advanced(stage - 1, track[every], track0[every], curl)
        open_end = lax.axis_index("ax") == lax.axis_size("ax") - 1
        corner[every] = jnp.where(open_end, 0.0, value)
        curl = ahead[pl.ds(end, devs)] + track[pl.ds(3 * devs, devs)]
        corner[after] = advanced(stage - 1, track[after], track0[after], curl)

    def values(d, c, first):
        return [
            table_ref[offset_ref[d, first + k] + (c * devs + d) * per] for k in range(per)
        ]

    if stage == 0:

        @pl.loop(0, devs, unroll=UNROLL)
        def _(d):
            for c in (0, 2):
                own = values(d, c, per)
                for i in range(2):
                    src_ax_ref[pl.ds((c + i) * devs + d, 1)] = nu_ax_ref[pl.ds(nu_ax + c + i, 1)] * picked(
                        nu_ax_ref[pl.ds(nu_ax + 4 + i, 1)], own
                    )

    for at, own, sign in ((0, 2, 1.0), (1, 3, 1.0), (2, 0, -1.0), (3, 1, -1.0)):
        part = pl.ds(at * devs, devs)
        flux = ax_behind[part] + sign * mine[pl.ds(own * devs, devs)]
        if at == 3:
            flux = flux + corner[after]
        edge[part] = nu_ax_ref[pl.ds(nu_ax + at, 1)] * flux - src_ax_ref[part]
    if stage < 2:
        before = edge[every]
        minus[pl.ds(end, devs)] = before - radial_prev(before) - edge[pl.ds(2 * devs, devs)]
        next_track[pl.ds(0, 2 * devs)] = corner[...]
        next_track[pl.ds(3 * devs, devs)] = edge[pl.ds(3 * devs, devs)]

    @pl.loop(0, devs, unroll=UNROLL)
    def _(d):
        a = [[a_ref[d, c, i] for i in range(2)] for c in range(3)]
        up = [None, ahead[block(2 * d, height)], ahead[block(2 * d + 1, height)]]
        inten = [[None, None], [None, None], [None, None]]
        own = [values(d, c, per) for c in range(3)] if stage == 0 else None
        for i in range(2):
            next1 = a[1][1] if i == 0 else up[1]
            next2 = a[2][1] if i == 0 else up[2]
            row0 = ax_ahead[pl.ds(i * devs + d, 1)]
            row2 = ax_ahead[pl.ds((2 + i) * devs + d, 1)]
            flux = (
                (axial_next(a[2][i], row2) - a[2][i]) - (radial_next(a[1][i]) - a[1][i]),
                (radial_next(a[0][i]) - a[0][i]) - (next2 - a[2][i]),
                (next1 - a[1][i]) - (axial_next(a[0][i], row0) - a[0][i]),
            )
            for c in range(3):
                if stage == 0:
                    src = nu_ref[c, i] * picked(code_ref[i], own[c])
                    src_ref[d, c, i] = src
                else:
                    src = src_ref[d, c, i]
                inten[c][i] = nu_ref[c, i] * flux[c] - src
        back_src = [None, None]
        for c in range(1, 3):
            if stage == 0:
                src = nu_az_ref[block(2 * devs + 1 + c, height)] * picked(
                    nu_az_ref[pl.ds(nu_az + 2 * height, height)], values(d, c, 0)
                )
                src_az_ref[2 * d + c - 1] = src
            else:
                src = src_az_ref[2 * d + c - 1]
            back_src[c - 1] = src
        beyond = jnp.where(rows(a[1][0].shape) == top, corner[pl.ds(d, 1)], 0.0)
        back1 = nu_az_ref[pl.ds(nu_az, height)] * (behind[block(2 * d, height)] - a[2][0]) - back_src[0]
        back2 = (
            nu_az_ref[pl.ds(nu_az + height, height)]
            * (behind[block(2 * d + 1, height)] + a[1][0] - beyond)
            - back_src[1]
        )
        new = [[None, None], [None, None], [None, None]]
        for i in range(2):
            prev1 = back1 if i == 0 else inten[1][0]
            prev2 = back2 if i == 0 else inten[2][0]
            row0 = edge[pl.ds(i * devs + d, 1)]
            row2 = edge[pl.ds((2 + i) * devs + d, 1)]
            i0, i1, i2 = inten[0][i], inten[1][i], inten[2][i]
            curl = (
                (i2 - axial_prev(i2, row2)) - (i1 - radial_prev(i1)),
                (i0 - radial_prev(i0)) - (i2 - prev2),
                (i1 - prev1) - (i0 - axial_prev(i0, row0)),
            )
            for c in range(3):
                start = start_ref[d, c, i] if stage == 1 else None
                value = advanced(stage, a[c][i], start, curl[c])
                out_ref[d, c, i] = value
                new[c][i] = value
        if stage < 2:
            first1, first2 = back1[0:1], back2[0:1]
            ax_minus[pl.ds(4 * devs + d, 1)] = first2 - (first1 - radial_prev(first1))
            next_track[pl.ds(2 * devs + d, 1)] = back2[top:]
            pack_az(d, height, new, minus, plus)
            pack_ax(d, devs, new, ax_minus, ax_plus)

    if stage == 2:
        leave.wait()


def f32(*shape):
    return jax.ShapeDtypeStruct(shape, jnp.float32)


def shards(start_field, reluctivity, lamination, magnets, region_ids, pieces, slot_map):
    devs, comps, cells_az, cells_ax, radial = start_field.shape
    count_az = lax.axis_size("az")
    per = pieces.shape[2]
    whole = 2 * devs * cells_ax

    field_like = f32(*start_field.shape)
    edges = [
        f32(4 * devs, radial),
        f32(5 * devs + 8, radial),
        f32(*reluctivity.shape),
        f32(*lamination.shape),
        jax.ShapeDtypeStruct(slot_map.shape, jnp.int32),
    ]
    ax_minus, ax_plus, nu, code, offset = pl.pallas_call(
        functools.partial(edge_kernel, per),
        out_shape=edges,
        in_specs=[HBM] * 6,
        out_specs=[VMEM] * len(edges),
        scratch_shapes=[pltpu.VMEM(start_field.shape, jnp.float32)]
        + [pltpu.VMEM(lamination.shape, jnp.int32)] * 3
        + [pltpu.VMEM(slot_map.shape, jnp.int32), pltpu.SemaphoreType.DMA((7,))],
        compiler_params=pltpu.CompilerParams(vmem_limit_bytes=LIMIT_FIRST),
    )(start_field, reluctivity, lamination, magnets, region_ids, slot_map)
    ax_ahead, ax_behind = moved(ax_minus, 0, -1), moved(ax_plus, 0, 1)
    planes = [f32(whole + devs, radial), f32(whole + devs + 3 * cells_ax, radial)]
    packed = pl.pallas_call(
        plane_kernel,
        out_shape=planes,
        in_specs=[VMEM] * 3,
        out_specs=[VMEM] * 2,
        compiler_params=pltpu.CompilerParams(vmem_limit_bytes=LIMIT),
        cost_estimate=pl.CostEstimate(flops=10**7, bytes_accessed=3 * MIB, transcendentals=0),
    )(start_field, nu, code)
    minus, plus = pl.pallas_call(
        functools.partial(corner_kernel, devs),
        out_shape=planes,
        in_specs=[VMEM, VMEM, ANY, ANY],
        out_specs=[ANY] * 2,
        scratch_shapes=[pltpu.SemaphoreType.DMA((2,))],
        input_output_aliases={2: 0, 3: 1},
        compiler_params=pltpu.CompilerParams(vmem_limit_bytes=LIMIT),
    )(ax_ahead, ax_behind, *packed)
    halos = (moved(minus, -1, 0), moved(plus, 1, 0), ax_ahead, ax_behind, ax_minus)
    flat = pieces.reshape(1, comps * devs * per)
    table = lax.all_to_all(
        jnp.broadcast_to(flat, (count_az, comps * devs * per)), "az", 0, 0, tiled=True
    ).reshape(-1)
    nu_az, nu_ax = halos[1], halos[3]

    def exchange(minus, plus, ax_minus, ax_plus):
        ahead, behind = moved(minus, -1, 0), moved(plus, 1, 0)
        return ahead, behind, moved(ax_minus, 0, -1), moved(ax_plus, 0, 1), ax_minus

    def step(stage, field, halos, more, more_specs):
        outs = [field_like]
        if stage < 2:
            outs += [
                f32(whole + devs, radial),
                f32(whole, radial),
                f32(5 * devs, radial),
                f32(4 * devs, radial),
                f32(4 * devs, radial),
            ]
        else:
            outs += [field_like]
        if stage == 0:
            outs += [field_like, f32(2 * devs, cells_ax, radial), f32(4 * devs, radial)]
        return pl.pallas_call(
            functools.partial(step_kernel, stage, per),
            out_shape=outs,
            in_specs=[VMEM] * 9 + more_specs,
            out_specs=[VMEM] * len(outs) if stage < 2 else [VMEM, HBM],
            scratch_shapes=[
                pltpu.VMEM((4 * devs, radial), jnp.float32),
                pltpu.VMEM((2 * devs, radial), jnp.float32),
            ]
            + [pltpu.SemaphoreType.DMA] * (stage // 2),
            compiler_params=pltpu.CompilerParams(vmem_limit_bytes=LIMIT),
        )(field, nu, nu_az, nu_ax, *halos, *more)

    middle, *rest = step(0, start_field, halos, [code, offset, table], [VMEM, SMEM, SMEM])
    packed, track0, src = rest[:4], rest[4], rest[5:]
    final, *rest = step(1, middle, exchange(*packed), [*src, track0, start_field], [VMEM] * 5)
    packed, track1 = rest[:4], rest[4]
    residual, out = step(2, final, exchange(*packed), [*src, track0, track1], [VMEM] * 5)
    return out, residual


def solution(mesh):
    placed = (
        P(None, None, "az", "ax", None),
        P(None, "az", "ax", None),
        P("az", "ax", None),
        P("az", "ax", None),
        P("az", "ax", None),
        P(None, None, "az"),
        P(),
    )
    return jax.shard_map(
        shards,
        mesh=mesh,
        in_specs=placed,
        out_specs=(P(None, None, "az", "ax", None), P(None, None, "az", "ax", None)),
        check_vma=False,
    )
```

```python
import functools

import jax
import jax.numpy as jnp
from jax import lax
from jax.experimental import pallas as pl
from jax.experimental.pallas import tpu as pltpu
from jax.sharding import PartitionSpec as P

mass_term = 1.0
cheb_centre = 8.5
cheb_halfwidth = 7.5
cheb_sigma = cheb_centre / cheb_halfwidth
rho_first = 1.0 / cheb_sigma
rho_second = 1.0 / (2.0 * cheb_sigma - rho_first)

mix_second = rho_second * rho_first
step_second = 2.0 * rho_second / cheb_halfwidth

VMEM = pl.BlockSpec(memory_space=pltpu.VMEM)
SMEM = pl.BlockSpec(memory_space=pltpu.SMEM)
HBM = pl.BlockSpec(memory_space=pltpu.HBM)
ANY = pl.BlockSpec(memory_space=pl.ANY)
MIB = 1024 * 1024
LIMIT = 16 * MIB
UNROLL = 4
LIMIT_FIRST = 63 * MIB


def moved(value, shift_az, shift_ax):
    count_az, count_ax = lax.axis_size("az"), lax.axis_size("ax")
    pairs = [
        (a * count_ax + q, (a + shift_az) % count_az * count_ax + q + shift_ax)
        for a in range(count_az)
        for q in range(count_ax)
        if 0 <= q + shift_ax < count_ax
    ]
    return lax.ppermute(value, ("az", "ax"), pairs)


def swapped(value, odd):
    count_az, count_ax = lax.axis_size("az"), lax.axis_size("ax")
    pairs = [
        (a * count_ax + q, (a + (1 if a % 2 == odd else -1)) % count_az * count_ax + q)
        for a in range(count_az)
        for q in range(count_ax)
    ]
    return lax.ppermute(value, ("az", "ax"), pairs)


def by_parity(body, far, near):
    parity = lax.rem(lax.axis_index("az"), 2)

    @pl.when(parity == 0)
    def _():
        body(near, far)

    @pl.when(parity == 1)
    def _():
        body(far, near)


def lanes(shape):
    return lax.broadcasted_iota(jnp.int32, shape, 1)


def rows(shape):
    return lax.broadcasted_iota(jnp.int32, shape, 0)


def radial_next(v):
    tile = 128
    rolled = [pltpu.roll(v[:, at : at + tile], tile - 1, 1) for at in range(0, v.shape[1], tile)]
    last = lanes(rolled[0].shape) == tile - 1
    rolled.append(jnp.zeros_like(rolled[0]))
    return jnp.concatenate(
        [jnp.where(last, later, part) for part, later in zip(rolled, rolled[1:])], axis=1
    )


def radial_prev(v):
    tile = 128
    rolled = [pltpu.roll(v[:, at : at + tile], 1, 1) for at in range(0, v.shape[1], tile)]
    first = lanes(rolled[0].shape) == 0
    rolled.insert(0, jnp.zeros_like(rolled[0]))
    return jnp.concatenate(
        [jnp.where(first, sooner, part) for sooner, part in zip(rolled, rolled[1:])], axis=1
    )


def axial_next(v, row):
    n = v.shape[0]
    return jnp.where(rows(v.shape) == n - 1, row, pltpu.roll(v, n - 1, 0))


def axial_prev(v, row):
    return jnp.where(rows(v.shape) == 0, row, pltpu.roll(v, 1, 0))


def block(k, height):
    return pl.ds(pl.multiple_of(k * height, height), height)


def pack_az(d, height, a, minus, plus):
    minus[block(2 * d, height)] = a[1][0]
    minus[block(2 * d + 1, height)] = a[2][0]
    plus[block(2 * d, height)] = radial_next(a[0][1]) - a[0][1] + a[2][1]
    plus[block(2 * d + 1, height)] = a[0][1] - axial_next(a[0][1], 0.0) - a[1][1]


def pack_ax(d, devs, a, ax_minus, ax_plus):
    top = a[0][0].shape[0] - 1
    for i in range(2):
        ax_minus[pl.ds(i * devs + d, 1)] = a[0][i][0:1]
        ax_minus[pl.ds((2 + i) * devs + d, 1)] = a[2][i][0:1]
        end = a[1][i][top:]
        ax_plus[pl.ds(i * devs + d, 1)] = end - radial_next(end) - a[2][i][top:]
    ax_plus[pl.ds(2 * devs + d, 1)] = a[1][1][top:] - a[1][0][top:] + a[0][0][top:]
    ax_plus[pl.ds(3 * devs + d, 1)] = a[0][1][top:] - a[1][1][top:]


def edge_kernel(
    per, a_hbm, reluct_hbm, lam_hbm, mag_hbm, reg_hbm, slots_hbm,
    ax_minus, ax_plus, nu_ref, code_ref, offset_ref,
    a_ref, lam_ref, mag_ref, reg_ref, slots_ref, sems,
):
    devs = a_ref.shape[0]
    top = a_ref.shape[3] - 1
    parts = 2
    some = devs // parts
    copies = [
        pltpu.make_async_copy(reluct_hbm, nu_ref, sems.at[0]),
        pltpu.make_async_copy(lam_hbm, lam_ref, sems.at[1]),
        pltpu.make_async_copy(mag_hbm, mag_ref, sems.at[2]),
        pltpu.make_async_copy(reg_hbm, reg_ref, sems.at[3]),
        pltpu.make_async_copy(slots_hbm, slots_ref, sems.at[4]),
    ]
    for part in range(parts):
        at = pl.ds(part * some, some)
        copies.append(pltpu.make_async_copy(a_hbm.at[at], a_ref.at[at], sems.at[5 + part]))
    for copy in copies:
        copy.start()
    for copy in copies[:5]:
        copy.wait()

    base = lax.axis_index("az") * per
    slots = slots_ref[...]
    count = slots.shape[1]
    slots = pltpu.roll(slots, lax.rem(2 * count - base + per, count), 1)
    row = lax.div(slots, jnp.int32(per))
    offset_ref[...] = row * (3 * devs * per) + (slots - row * per)
    for i in range(2):
        nu_ref[1, i] = nu_ref[1, i] * (1.0 + 3.0 * lam_ref[i].astype(jnp.float32))
        code_ref[i] = jnp.where(mag_ref[i] == 1, reg_ref[i] - base + 1, 0).astype(jnp.float32)
    for i in range(2):
        at = 5 * devs + i
        ax_plus[pl.ds(at, 1)] = nu_ref[0, i, top:]
        ax_plus[pl.ds(at + 2, 1)] = nu_ref[2, i, top:]
        ax_plus[pl.ds(at + 4, 1)] = code_ref[i, top:]
        ax_plus[pl.ds(at + 6, 1)] = jnp.zeros_like(code_ref[i, top:])

    for part in range(parts):
        copies[5 + part].wait()

        @pl.loop(part * some, (part + 1) * some, unroll=UNROLL)
        def _(d):
            a = [[a_ref[d, c, i] for i in range(2)] for c in range(3)]
            pack_ax(d, devs, a, ax_minus, ax_plus)
            ax_plus[pl.ds(4 * devs + d, 1)] = a[1][0][top:]


def plane_kernel(a_ref, nu_ref, code_ref, far, near):
    devs, height = a_ref.shape[0], a_ref.shape[3]
    end = 2 * devs * height + devs

    def body(plus, minus):
        plus[pl.ds(end, height)] = nu_ref[1, 1]
        plus[pl.ds(end + height, height)] = nu_ref[2, 1]
        plus[pl.ds(end + 2 * height, height)] = code_ref[1]

        @pl.loop(0, devs, unroll=UNROLL)
        def _(d):
            a = [[a_ref[d, c, i] for i in range(2)] for c in range(3)]
            pack_az(d, height, a, minus, plus)

    by_parity(body, far, near)


def corner_kernel(end, devs, ax_ahead, ax_behind, far_in, near_in, far, near, sems):
    at = pl.ds(end, devs)

    def body(plus, minus):
        copies = [
            pltpu.make_async_copy(ax_behind.at[pl.ds(4 * devs, devs)], minus.at[at], sems.at[0]),
            pltpu.make_async_copy(ax_ahead.at[pl.ds(devs, devs)], plus.at[at], sems.at[1]),
        ]
        for copy in copies:
            copy.start()
        for copy in copies:
            copy.wait()

    by_parity(body, far, near)


def picked(code, values):
    out = jnp.zeros_like(code)
    for k, value in enumerate(values):
        out = jnp.where(code == k + 1.0, value, out)
    return out


def advanced(stage, value, start, curl):
    if stage == 0:
        return value * (1.0 - mass_term / cheb_centre) - curl * (1.0 / cheb_centre)
    if stage == 1:
        return (
            value * (1.0 + mix_second - mass_term * step_second) - start * mix_second - curl * step_second
        )
    return -curl - mass_term * value


def step_kernel(stage, per, *refs):
    refs = list(refs)
    halo = [refs.pop(4), refs.pop(4)]
    statics = refs.pop(2), refs.pop(2)
    sent = [None, None]
    if stage < 2:
        first = (10, 12)[stage]
        sent = [refs.pop(first), refs.pop(first)]

    def body(plus, minus):
        step_body(stage, per, refs, plus, minus)

    by_parity(body, (halo[0], statics[0], sent[0]), (halo[1], statics[1], sent[1]))


def step_body(stage, per, refs, beyond_refs, behind_refs):
    it = iter(refs)
    ahead, _, plus = beyond_refs
    behind, nu_az_ref, minus = behind_refs
    a_ref, nu_ref, nu_ax_ref = next(it), next(it), next(it)
    ax_ahead, ax_behind, mine = [next(it) for _ in range(3)]
    if stage == 0:
        code_ref, offset_ref, table_ref = next(it), next(it), next(it)
    else:
        src_ref, src_az_ref, src_ax_ref, track0 = [next(it) for _ in range(4)]
    track = track0 if stage == 1 else None
    if stage == 1:
        start_ref = next(it)
    if stage == 2:
        track = next(it)
    out_ref = next(it)
    if stage < 2:
        ax_minus, ax_plus, next_track = [next(it) for _ in range(3)]
    if stage == 0:
        src_ref, src_az_ref, src_ax_ref = next(it), next(it), next(it)
    if stage == 2:
        final_hbm = next(it)
    edge, corner = next(it), next(it)
    if stage == 2:
        leave = pltpu.make_async_copy(a_ref, final_hbm, next(it))
        leave.start()
    devs, height = a_ref.shape[0], a_ref.shape[3]
    top = height - 1
    end = 2 * devs * height
    nu_az = end + devs
    nu_ax = 5 * devs
    every = pl.ds(0, devs)
    after = pl.ds(devs, devs)

    if stage == 0:
        corner[every] = behind[pl.ds(end, devs)]
        corner[after] = ahead[pl.ds(end, devs)]
    else:
        curl = ax_ahead[pl.ds(4 * devs, devs)] - track[pl.ds(2 * devs, devs)]
        value = advanced(stage - 1, track[every], track0[every], curl)
        open_end = lax.axis_index("ax") == lax.axis_size("ax") - 1
        corner[every] = jnp.where(open_end, 0.0, value)
        curl = ahead[pl.ds(end, devs)] + track[pl.ds(3 * devs, devs)]
        corner[after] = advanced(stage - 1, track[after], track0[after], curl)

    def values(d, c, first):
        return [
            table_ref[offset_ref[d, first + k] + (c * devs + d) * per] for k in range(per)
        ]

    if stage == 0:

        @pl.loop(0, devs, unroll=UNROLL)
        def _(d):
            for c in (0, 2):
                own = values(d, c, per)
                for i in range(2):
                    src_ax_ref[pl.ds((c + i) * devs + d, 1)] = nu_ax_ref[pl.ds(nu_ax + c + i, 1)] * picked(
                        nu_ax_ref[pl.ds(nu_ax + 4 + i, 1)], own
                    )

    for at, own, sign in ((0, 2, 1.0), (1, 3, 1.0), (2, 0, -1.0), (3, 1, -1.0)):
        part = pl.ds(at * devs, devs)
        flux = ax_behind[part] + sign * mine[pl.ds(own * devs, devs)]
        if at == 3:
            flux = flux + corner[after]
        edge[part] = nu_ax_ref[pl.ds(nu_ax + at, 1)] * flux - src_ax_ref[part]
    if stage < 2:
        before = edge[every]
        minus[pl.ds(end, devs)] = before - radial_prev(before) - edge[pl.ds(2 * devs, devs)]
        next_track[pl.ds(0, 2 * devs)] = corner[...]
        next_track[pl.ds(3 * devs, devs)] = edge[pl.ds(3 * devs, devs)]

    @pl.loop(0, devs, unroll=UNROLL)
    def _(d):
        a = [[a_ref[d, c, i] for i in range(2)] for c in range(3)]
        up = [None, ahead[block(2 * d, height)], ahead[block(2 * d + 1, height)]]
        inten = [[None, None], [None, None], [None, None]]
        own = [values(d, c, per) for c in range(3)] if stage == 0 else None
        for i in range(2):
            next1 = a[1][1] if i == 0 else up[1]
            next2 = a[2][1] if i == 0 else up[2]
            row0 = ax_ahead[pl.ds(i * devs + d, 1)]
            row2 = ax_ahead[pl.ds((2 + i) * devs + d, 1)]
            flux = (
                (axial_next(a[2][i], row2) - a[2][i]) - (radial_next(a[1][i]) - a[1][i]),
                (radial_next(a[0][i]) - a[0][i]) - (next2 - a[2][i]),
                (next1 - a[1][i]) - (axial_next(a[0][i], row0) - a[0][i]),
            )
            for c in range(3):
                if stage == 0:
                    src = nu_ref[c, i] * picked(code_ref[i], own[c])
                    src_ref[d, c, i] = src
                else:
                    src = src_ref[d, c, i]
                inten[c][i] = nu_ref[c, i] * flux[c] - src
        back_src = [None, None]
        for c in range(1, 3):
            if stage == 0:
                src = nu_az_ref[block(2 * devs + 1 + c, height)] * picked(
                    nu_az_ref[pl.ds(nu_az + 2 * height, height)], values(d, c, 0)
                )
                src_az_ref[2 * d + c - 1] = src
            else:
                src = src_az_ref[2 * d + c - 1]
            back_src[c - 1] = src
        beyond = jnp.where(rows(a[1][0].shape) == top, corner[pl.ds(d, 1)], 0.0)
        back1 = nu_az_ref[pl.ds(nu_az, height)] * (behind[block(2 * d, height)] - a[2][0]) - back_src[0]
        back2 = (
            nu_az_ref[pl.ds(nu_az + height, height)]
            * (behind[block(2 * d + 1, height)] + a[1][0] - beyond)
            - back_src[1]
        )
        new = [[None, None], [None, None], [None, None]]
        for i in range(2):
            prev1 = back1 if i == 0 else inten[1][0]
            prev2 = back2 if i == 0 else inten[2][0]
            row0 = edge[pl.ds(i * devs + d, 1)]
            row2 = edge[pl.ds((2 + i) * devs + d, 1)]
            i0, i1, i2 = inten[0][i], inten[1][i], inten[2][i]
            curl = (
                (i2 - axial_prev(i2, row2)) - (i1 - radial_prev(i1)),
                (i0 - radial_prev(i0)) - (i2 - prev2),
                (i1 - prev1) - (i0 - axial_prev(i0, row0)),
            )
            for c in range(3):
                start = start_ref[d, c, i] if stage == 1 else None
                value = advanced(stage, a[c][i], start, curl[c])
                out_ref[d, c, i] = value
                new[c][i] = value
        if stage < 2:
            first1, first2 = back1[0:1], back2[0:1]
            ax_minus[pl.ds(4 * devs + d, 1)] = first2 - (first1 - radial_prev(first1))
            next_track[pl.ds(2 * devs + d, 1)] = back2[top:]
            pack_az(d, height, new, minus, plus)
            pack_ax(d, devs, new, ax_minus, ax_plus)

    if stage == 2:
        leave.wait()


def f32(*shape):
    return jax.ShapeDtypeStruct(shape, jnp.float32)


def shards(start_field, reluctivity, lamination, magnets, region_ids, pieces, slot_map):
    devs, comps, cells_az, cells_ax, radial = start_field.shape
    count_az = lax.axis_size("az")
    per = pieces.shape[2]
    whole = 2 * devs * cells_ax

    field_like = f32(*start_field.shape)
    edges = [
        f32(4 * devs, radial),
        f32(5 * devs + 8, radial),
        f32(*reluctivity.shape),
        f32(*lamination.shape),
        jax.ShapeDtypeStruct(slot_map.shape, jnp.int32),
    ]
    ax_minus, ax_plus, nu, code, offset = pl.pallas_call(
        functools.partial(edge_kernel, per),
        out_shape=edges,
        in_specs=[HBM] * 6,
        out_specs=[VMEM] * len(edges),
        scratch_shapes=[pltpu.VMEM(start_field.shape, jnp.float32)]
        + [pltpu.VMEM(lamination.shape, jnp.int32)] * 3
        + [pltpu.VMEM(slot_map.shape, jnp.int32), pltpu.SemaphoreType.DMA((7,))],
        compiler_params=pltpu.CompilerParams(vmem_limit_bytes=LIMIT_FIRST),
    )(start_field, reluctivity, lamination, magnets, region_ids, slot_map)
    ax_ahead, ax_behind = moved(ax_minus, 0, -1), moved(ax_plus, 0, 1)
    planes = [f32(whole + devs + 3 * cells_ax, radial)] * 2
    packed = pl.pallas_call(
        plane_kernel,
        out_shape=planes,
        in_specs=[VMEM] * 3,
        out_specs=[VMEM] * 2,
        compiler_params=pltpu.CompilerParams(vmem_limit_bytes=LIMIT),
        cost_estimate=pl.CostEstimate(flops=10**7, bytes_accessed=3 * MIB, transcendentals=0),
    )(start_field, nu, code)
    far, near = pl.pallas_call(
        functools.partial(corner_kernel, whole, devs),
        out_shape=planes,
        in_specs=[VMEM, VMEM, ANY, ANY],
        out_specs=[ANY] * 2,
        scratch_shapes=[pltpu.SemaphoreType.DMA((2,))],
        input_output_aliases={2: 0, 3: 1},
        compiler_params=pltpu.CompilerParams(vmem_limit_bytes=LIMIT),
    )(ax_ahead, ax_behind, *packed)
    far_halo, near_halo = swapped(far, 1), swapped(near, 0)
    halos = (far_halo, near_halo, ax_ahead, ax_behind, ax_minus)
    flat = pieces.reshape(1, comps * devs * per)
    table = lax.all_to_all(
        jnp.broadcast_to(flat, (count_az, comps * devs * per)), "az", 0, 0, tiled=True
    ).reshape(-1)

    def exchange(far, near, ax_minus, ax_plus):
        from_far, from_near = swapped(far, 1), swapped(near, 0)
        return from_far, from_near, moved(ax_minus, 0, -1), moved(ax_plus, 0, 1), ax_minus

    def step(stage, field, halos, more, more_specs):
        outs = [field_like]
        if stage < 2:
            outs += [
                f32(whole + devs, radial),
                f32(whole + devs, radial),
                f32(5 * devs, radial),
                f32(4 * devs, radial),
                f32(4 * devs, radial),
            ]
        else:
            outs += [field_like]
        if stage == 0:
            outs += [field_like, f32(2 * devs, cells_ax, radial), f32(4 * devs, radial)]
        return pl.pallas_call(
            functools.partial(step_kernel, stage, per),
            out_shape=outs,
            in_specs=[VMEM] * 10 + more_specs,
            out_specs=[VMEM] * len(outs) if stage < 2 else [VMEM, HBM],
            scratch_shapes=[
                pltpu.VMEM((4 * devs, radial), jnp.float32),
                pltpu.VMEM((2 * devs, radial), jnp.float32),
            ]
            + [pltpu.SemaphoreType.DMA] * (stage // 2),
            compiler_params=pltpu.CompilerParams(vmem_limit_bytes=LIMIT),
        )(field, nu, far_halo, near_halo, *halos[:2], ax_behind, *halos[2:], *more)

    middle, *rest = step(0, start_field, halos, [code, offset, table], [VMEM, SMEM, SMEM])
    packed, track0, src = rest[:4], rest[4], rest[5:]
    final, *rest = step(1, middle, exchange(*packed), [*src, track0, start_field], [VMEM] * 5)
    packed, track1 = rest[:4], rest[4]
    residual, out = step(2, final, exchange(*packed), [*src, track0, track1], [VMEM] * 5)
    return out, residual


def solution(mesh):
    placed = (
        P(None, None, "az", "ax", None),
        P(None, "az", "ax", None),
        P("az", "ax", None),
        P("az", "ax", None),
        P("az", "ax", None),
        P(None, None, "az"),
        P(),
    )
    return jax.shard_map(
        shards,
        mesh=mesh,
        in_specs=placed,
        out_specs=(P(None, None, "az", "ax", None), P(None, None, "az", "ax", None)),
        check_vma=False,
    )
```

```python
import functools

import jax
import jax.numpy as jnp
from jax import lax
from jax.experimental import pallas as pl
from jax.experimental.pallas import tpu as pltpu
from jax.sharding import PartitionSpec as P

mass_term = 1.0
cheb_centre = 8.5
cheb_halfwidth = 7.5
cheb_sigma = cheb_centre / cheb_halfwidth
rho_first = 1.0 / cheb_sigma
rho_second = 1.0 / (2.0 * cheb_sigma - rho_first)

mix_second = rho_second * rho_first
step_second = 2.0 * rho_second / cheb_halfwidth

VMEM = pl.BlockSpec(memory_space=pltpu.VMEM)
SMEM = pl.BlockSpec(memory_space=pltpu.SMEM)
HBM = pl.BlockSpec(memory_space=pltpu.HBM)
ANY = pl.BlockSpec(memory_space=pl.ANY)
MIB = 1024 * 1024
LIMIT = 16 * MIB
UNROLL = 4
LIMIT_FIRST = 63 * MIB


def moved(value, shift_az, shift_ax):
    count_az, count_ax = lax.axis_size("az"), lax.axis_size("ax")
    pairs = [
        (a * count_ax + q, (a + shift_az) % count_az * count_ax + q + shift_ax)
        for a in range(count_az)
        for q in range(count_ax)
        if 0 <= q + shift_ax < count_ax
    ]
    return lax.ppermute(value, ("az", "ax"), pairs)


def swapped(value, odd):
    count_az, count_ax = lax.axis_size("az"), lax.axis_size("ax")
    pairs = [
        (a * count_ax + q, (a + (1 if a % 2 == odd else -1)) % count_az * count_ax + q)
        for a in range(count_az)
        for q in range(count_ax)
    ]
    return lax.ppermute(value, ("az", "ax"), pairs)


def swapped_ax(value, odd):
    count = lax.axis_size("ax")
    pairs = [(q, q + (1 if q % 2 == odd else -1)) for q in range(count)]
    return lax.ppermute(value, "ax", [(q, to) for q, to in pairs if 0 <= to < count])


def by_parity(axis, body, far, near):
    parity = lax.rem(lax.axis_index(axis), 2)

    @pl.when(parity == 0)
    def _():
        body(near, far)

    @pl.when(parity == 1)
    def _():
        body(far, near)


def lanes(shape):
    return lax.broadcasted_iota(jnp.int32, shape, 1)


def rows(shape):
    return lax.broadcasted_iota(jnp.int32, shape, 0)


def radial_next(v):
    tile = 128
    rolled = [pltpu.roll(v[:, at : at + tile], tile - 1, 1) for at in range(0, v.shape[1], tile)]
    last = lanes(rolled[0].shape) == tile - 1
    rolled.append(jnp.zeros_like(rolled[0]))
    return jnp.concatenate(
        [jnp.where(last, later, part) for part, later in zip(rolled, rolled[1:])], axis=1
    )


def radial_prev(v):
    tile = 128
    rolled = [pltpu.roll(v[:, at : at + tile], 1, 1) for at in range(0, v.shape[1], tile)]
    first = lanes(rolled[0].shape) == 0
    rolled.insert(0, jnp.zeros_like(rolled[0]))
    return jnp.concatenate(
        [jnp.where(first, sooner, part) for sooner, part in zip(rolled, rolled[1:])], axis=1
    )


def axial_next(v, row):
    n = v.shape[0]
    return jnp.where(rows(v.shape) == n - 1, row, pltpu.roll(v, n - 1, 0))


def axial_prev(v, row):
    return jnp.where(rows(v.shape) == 0, row, pltpu.roll(v, 1, 0))


def block(k, height):
    return pl.ds(pl.multiple_of(k * height, height), height)


def pack_az(d, height, a, minus, plus):
    minus[block(2 * d, height)] = a[1][0]
    minus[block(2 * d + 1, height)] = a[2][0]
    plus[block(2 * d, height)] = radial_next(a[0][1]) - a[0][1] + a[2][1]
    plus[block(2 * d + 1, height)] = a[0][1] - axial_next(a[0][1], 0.0) - a[1][1]


def pack_ax(d, devs, a, ax_minus, ax_plus):
    top = a[0][0].shape[0] - 1
    for i in range(2):
        ax_minus[pl.ds(i * devs + d, 1)] = a[0][i][0:1]
        ax_minus[pl.ds((2 + i) * devs + d, 1)] = a[2][i][0:1]
        end = a[1][i][top:]
        ax_plus[pl.ds(i * devs + d, 1)] = end - radial_next(end) - a[2][i][top:]
    ax_plus[pl.ds(2 * devs + d, 1)] = a[1][1][top:] - a[1][0][top:] + a[0][0][top:]
    ax_plus[pl.ds(3 * devs + d, 1)] = a[0][1][top:] - a[1][1][top:]


def edge_kernel(
    per, a_hbm, reluct_hbm, lam_hbm, mag_hbm, reg_hbm, slots_hbm,
    ax_far, ax_near, nu_ref, code_ref, offset_ref,
    a_ref, lam_ref, mag_ref, reg_ref, slots_ref, sems,
):
    devs = a_ref.shape[0]
    top = a_ref.shape[3] - 1
    parts = 2
    some = devs // parts
    copies = [
        pltpu.make_async_copy(reluct_hbm, nu_ref, sems.at[0]),
        pltpu.make_async_copy(lam_hbm, lam_ref, sems.at[1]),
        pltpu.make_async_copy(mag_hbm, mag_ref, sems.at[2]),
        pltpu.make_async_copy(reg_hbm, reg_ref, sems.at[3]),
        pltpu.make_async_copy(slots_hbm, slots_ref, sems.at[4]),
    ]
    for part in range(parts):
        at = pl.ds(part * some, some)
        copies.append(pltpu.make_async_copy(a_hbm.at[at], a_ref.at[at], sems.at[5 + part]))
    for copy in copies:
        copy.start()
    for copy in copies[:5]:
        copy.wait()

    base = lax.axis_index("az") * per
    slots = slots_ref[...]
    count = slots.shape[1]
    slots = pltpu.roll(slots, lax.rem(2 * count - base + per, count), 1)
    row = lax.div(slots, jnp.int32(per))
    offset_ref[...] = row * (3 * devs * per) + (slots - row * per)
    for i in range(2):
        nu_ref[1, i] = nu_ref[1, i] * (1.0 + 3.0 * lam_ref[i].astype(jnp.float32))
        code_ref[i] = jnp.where(mag_ref[i] == 1, reg_ref[i] - base, -1).astype(jnp.float32)
    for part in range(parts):
        copies[5 + part].wait()

    def body(ax_plus, ax_minus):
        for i in range(2):
            at = 5 * devs + i
            ax_plus[pl.ds(at, 1)] = nu_ref[0, i, top:]
            ax_plus[pl.ds(at + 2, 1)] = nu_ref[2, i, top:]
            ax_plus[pl.ds(at + 4, 1)] = code_ref[i, top:]
            ax_plus[pl.ds(at + 6, 1)] = jnp.zeros_like(code_ref[i, top:])

        @pl.loop(0, devs, unroll=UNROLL)
        def _(d):
            a = [[a_ref[d, c, i] for i in range(2)] for c in range(3)]
            pack_ax(d, devs, a, ax_minus, ax_plus)
            ax_plus[pl.ds(4 * devs + d, 1)] = a[1][0][top:]

    by_parity("ax", body, ax_far, ax_near)


def plane_kernel(a_ref, far, near):
    devs, height = a_ref.shape[0], a_ref.shape[3]

    def body(plus, minus):
        @pl.loop(0, devs, unroll=UNROLL)
        def _(d):
            a = [[a_ref[d, c, i] for i in range(2)] for c in range(3)]
            pack_az(d, height, a, minus, plus)

    by_parity("az", body, far, near)


def corner_kernel(end, devs, ax_far, ax_near, nu, code, far_in, near_in, far, near, sems):
    at = pl.ds(end, devs)
    height = nu.shape[2]

    def body_ax(ax_ahead, ax_behind):
        def body(plus, minus):
            copies = [
                (ax_behind.at[pl.ds(4 * devs, devs)], minus.at[at]),
                (ax_ahead.at[pl.ds(devs, devs)], plus.at[at]),
            ]
            for k, source in enumerate((nu.at[1, 1], nu.at[2, 1], code.at[1])):
                copies.append((source, plus.at[pl.ds(end + devs + k * height, height)]))
            copies = [
                pltpu.make_async_copy(source, to, sems.at[k]) for k, (source, to) in enumerate(copies)
            ]
            for copy in copies:
                copy.start()
            for copy in copies:
                copy.wait()

        by_parity("az", body, far, near)

    by_parity("ax", body_ax, ax_far, ax_near)


def settle_kernel(halo_far, halo_near, a_ref, ahead, behind, minus):
    devs = a_ref.shape[0]

    def body(ahead_ref, behind_ref):
        ahead[...] = ahead_ref[pl.ds(0, ahead.shape[0])]
        behind[...] = behind_ref[...]

    by_parity("ax", body, halo_far, halo_near)
    for d in range(devs):
        for i in range(2):
            minus[i * devs + d : i * devs + d + 1] = a_ref[d, 0, i, 0:1]
            minus[(2 + i) * devs + d : (2 + i) * devs + d + 1] = a_ref[d, 2, i, 0:1]


def picked(nu, code, values):
    rest, weight = code, 1
    while weight < len(values):
        weight *= 2
    values = list(values) + [values[-1]] * (weight - len(values))
    while len(values) > 1:
        weight //= 2
        high = rest > weight - 0.5
        rest = jnp.where(high, rest - weight, rest)
        half = len(values) // 2
        values = [jnp.where(high, b, a) for a, b in zip(values[:half], values[half:])]
    return jnp.where(code > -0.5, nu * values[0], 0.0)


def advanced(stage, value, start, curl):
    if stage == 0:
        return value * (1.0 - mass_term / cheb_centre) - curl * (1.0 / cheb_centre)
    if stage == 1:
        return (
            value * (1.0 + mix_second - mass_term * step_second) - start * mix_second - curl * step_second
        )
    return -curl - mass_term * value


def step_kernel(stage, per, *refs):
    refs = list(refs)
    halo = [refs.pop(4), refs.pop(4)]
    statics = refs.pop(2), refs.pop(2)
    sent = [None, None]
    if stage < 2:
        first = (10, 12)[stage]
        sent = [refs.pop(first), refs.pop(first)]

    def body(plus, minus):
        step_body(stage, per, refs, plus, minus)

    by_parity("az", body, (halo[0], statics[0], sent[0]), (halo[1], statics[1], sent[1]))


def step_body(stage, per, refs, beyond_refs, behind_refs):
    it = iter(refs)
    ahead, _, plus = beyond_refs
    behind, nu_az_ref, minus = behind_refs
    a_ref, nu_ref, nu_ax_ref = next(it), next(it), next(it)
    ax_ahead, ax_behind, mine = [next(it) for _ in range(3)]
    if stage == 0:
        code_ref, offset_ref, table_ref = next(it), next(it), next(it)
    else:
        src_ref, src_az_ref, src_ax_ref, track0 = [next(it) for _ in range(4)]
    track = track0 if stage == 1 else None
    if stage == 1:
        start_ref = next(it)
    if stage == 2:
        track = next(it)
    out_ref = next(it)
    if stage < 2:
        ax_minus, ax_plus, next_track = [next(it) for _ in range(3)]
    if stage == 0:
        src_ref, src_az_ref, src_ax_ref = next(it), next(it), next(it)
    if stage == 2:
        final_hbm = next(it)
    edge, corner = next(it), next(it)
    if stage == 2:
        res_hbm, out_ref, sems = out_ref, next(it), next(it)
        leave = pltpu.make_async_copy(a_ref, final_hbm, sems.at[0])
        leave.start()
    devs, height = a_ref.shape[0], a_ref.shape[3]
    top = height - 1
    end = 2 * devs * height
    nu_az = end + devs
    nu_ax = 5 * devs
    every = pl.ds(0, devs)
    after = pl.ds(devs, devs)

    if stage == 0:
        corner[every] = behind[pl.ds(end, devs)]
        corner[after] = ahead[pl.ds(end, devs)]
    else:
        curl = ax_ahead[pl.ds(4 * devs, devs)] - track[pl.ds(2 * devs, devs)]
        value = advanced(stage - 1, track[every], track0[every], curl)
        open_end = lax.axis_index("ax") == lax.axis_size("ax") - 1
        corner[every] = jnp.where(open_end, 0.0, value)
        curl = ahead[pl.ds(end, devs)] + track[pl.ds(3 * devs, devs)]
        corner[after] = advanced(stage - 1, track[after], track0[after], curl)

    def values(d, c, first):
        return [
            table_ref[offset_ref[d, first + k] + (c * devs + d) * per] for k in range(per)
        ]

    if stage == 0:

        @pl.loop(0, devs, unroll=UNROLL)
        def _(d):
            for c in (0, 2):
                own = values(d, c, per)
                for i in range(2):
                    src_ax_ref[pl.ds((c + i) * devs + d, 1)] = picked(
                        nu_ax_ref[pl.ds(nu_ax + c + i, 1)], nu_ax_ref[pl.ds(nu_ax + 4 + i, 1)], own
                    )

    for at, own, sign in ((0, 2, 1.0), (1, 3, 1.0), (2, 0, -1.0), (3, 1, -1.0)):
        part = pl.ds(at * devs, devs)
        flux = ax_behind[part] + sign * mine[pl.ds(own * devs, devs)]
        if at == 3:
            flux = flux + corner[after]
        edge[part] = nu_ax_ref[pl.ds(nu_ax + at, 1)] * flux - src_ax_ref[part]
    if stage < 2:
        before = edge[every]
        minus[pl.ds(end, devs)] = before - radial_prev(before) - edge[pl.ds(2 * devs, devs)]
        next_track[pl.ds(0, 2 * devs)] = corner[...]
        next_track[pl.ds(3 * devs, devs)] = edge[pl.ds(3 * devs, devs)]

    @pl.loop(0, devs, unroll=UNROLL)
    def _(d):
        a = [[a_ref[d, c, i] for i in range(2)] for c in range(3)]
        up = [None, ahead[block(2 * d, height)], ahead[block(2 * d + 1, height)]]
        inten = [[None, None], [None, None], [None, None]]
        own = [values(d, c, per) for c in range(3)] if stage == 0 else None
        for i in range(2):
            next1 = a[1][1] if i == 0 else up[1]
            next2 = a[2][1] if i == 0 else up[2]
            row0 = ax_ahead[pl.ds(i * devs + d, 1)]
            row2 = ax_ahead[pl.ds((2 + i) * devs + d, 1)]
            flux = (
                (axial_next(a[2][i], row2) - a[2][i]) - (radial_next(a[1][i]) - a[1][i]),
                (radial_next(a[0][i]) - a[0][i]) - (next2 - a[2][i]),
                (next1 - a[1][i]) - (axial_next(a[0][i], row0) - a[0][i]),
            )
            for c in range(3):
                if stage == 0:
                    src = picked(nu_ref[c, i], code_ref[i], own[c])
                    src_ref[d, c, i] = src
                else:
                    src = src_ref[d, c, i]
                inten[c][i] = nu_ref[c, i] * flux[c] - src
        back_src = [None, None]
        for c in range(1, 3):
            if stage == 0:
                src = picked(
                    nu_az_ref[pl.ds(nu_az + (c - 1) * height, height)],
                    nu_az_ref[pl.ds(nu_az + 2 * height, height)],
                    values(d, c, 0),
                )
                src_az_ref[2 * d + c - 1] = src
            else:
                src = src_az_ref[2 * d + c - 1]
            back_src[c - 1] = src
        beyond = jnp.where(rows(a[1][0].shape) == top, corner[pl.ds(d, 1)], 0.0)
        back1 = nu_az_ref[pl.ds(nu_az, height)] * (behind[block(2 * d, height)] - a[2][0]) - back_src[0]
        back2 = (
            nu_az_ref[pl.ds(nu_az + height, height)]
            * (behind[block(2 * d + 1, height)] + a[1][0] - beyond)
            - back_src[1]
        )
        new = [[None, None], [None, None], [None, None]]
        for i in range(2):
            prev1 = back1 if i == 0 else inten[1][0]
            prev2 = back2 if i == 0 else inten[2][0]
            row0 = edge[pl.ds(i * devs + d, 1)]
            row2 = edge[pl.ds((2 + i) * devs + d, 1)]
            i0, i1, i2 = inten[0][i], inten[1][i], inten[2][i]
            curl = (
                (i2 - axial_prev(i2, row2)) - (i1 - radial_prev(i1)),
                (i0 - radial_prev(i0)) - (i2 - prev2),
                (i1 - prev1) - (i0 - axial_prev(i0, row0)),
            )
            for c in range(3):
                start = start_ref[d, c, i] if stage == 1 else None
                value = advanced(stage, a[c][i], start, curl[c])
                out_ref[d, c, i] = value
                new[c][i] = value
        if stage == 2:
            pltpu.make_async_copy(out_ref.at[d], res_hbm.at[d], sems.at[1]).start()
        if stage < 2:
            first1, first2 = back1[0:1], back2[0:1]
            ax_minus[pl.ds(4 * devs + d, 1)] = first2 - (first1 - radial_prev(first1))
            next_track[pl.ds(2 * devs + d, 1)] = back2[top:]
            pack_az(d, height, new, minus, plus)
            pack_ax(d, devs, new, ax_minus, ax_plus)

    if stage == 2:
        leave.wait()
        pltpu.make_async_copy(out_ref, res_hbm, sems.at[1]).wait()


def f32(*shape):
    return jax.ShapeDtypeStruct(shape, jnp.float32)


def shards(start_field, reluctivity, lamination, magnets, region_ids, pieces, slot_map):
    devs, comps, cells_az, cells_ax, radial = start_field.shape
    count_az = lax.axis_size("az")
    per = pieces.shape[2]
    whole = 2 * devs * cells_ax

    field_like = f32(*start_field.shape)
    edges = [
        f32(5 * devs + 8, radial),
        f32(5 * devs + 8, radial),
        f32(*reluctivity.shape),
        f32(*lamination.shape),
        jax.ShapeDtypeStruct(slot_map.shape, jnp.int32),
    ]
    ax_far, ax_near, nu, code, offset = pl.pallas_call(
        functools.partial(edge_kernel, per),
        out_shape=edges,
        in_specs=[HBM] * 6,
        out_specs=[VMEM] * len(edges),
        scratch_shapes=[pltpu.VMEM(start_field.shape, jnp.float32)]
        + [pltpu.VMEM(lamination.shape, jnp.int32)] * 3
        + [pltpu.VMEM(slot_map.shape, jnp.int32), pltpu.SemaphoreType.DMA((7,))],
        compiler_params=pltpu.CompilerParams(vmem_limit_bytes=LIMIT_FIRST),
    )(start_field, reluctivity, lamination, magnets, region_ids, slot_map)
    ax_halos = swapped_ax(ax_far, 1), swapped_ax(ax_near, 0)
    planes = [f32(whole + devs + 3 * cells_ax, radial)] * 2
    packed = pl.pallas_call(
        plane_kernel,
        out_shape=planes,
        in_specs=[VMEM],
        out_specs=[VMEM] * 2,
        compiler_params=pltpu.CompilerParams(vmem_limit_bytes=LIMIT),
        cost_estimate=pl.CostEstimate(flops=10**7, bytes_accessed=3 * MIB, transcendentals=0),
    )(start_field)
    far, near = pl.pallas_call(
        functools.partial(corner_kernel, whole, devs),
        out_shape=planes,
        in_specs=[VMEM, VMEM, ANY, ANY, ANY, ANY],
        out_specs=[ANY] * 2,
        scratch_shapes=[pltpu.SemaphoreType.DMA((5,))],
        input_output_aliases={4: 0, 5: 1},
        compiler_params=pltpu.CompilerParams(vmem_limit_bytes=LIMIT),
    )(*ax_halos, nu, code, *packed)
    ax_ahead, ax_behind, ax_minus = pl.pallas_call(
        settle_kernel,
        out_shape=[f32(4 * devs, radial), f32(5 * devs + 8, radial), f32(4 * devs, radial)],
        in_specs=[VMEM] * 3,
        out_specs=[VMEM] * 3,
        compiler_params=pltpu.CompilerParams(vmem_limit_bytes=LIMIT),
    )(*ax_halos, start_field)
    far_halo, near_halo = swapped(far, 1), swapped(near, 0)
    halos = (far_halo, near_halo, ax_ahead, ax_behind, ax_minus)
    flat = pieces.reshape(1, comps * devs * per)
    table = lax.all_to_all(
        jnp.broadcast_to(flat, (count_az, comps * devs * per)), "az", 0, 0, tiled=True
    ).reshape(-1)

    def exchange(far, near, ax_minus, ax_plus):
        from_far, from_near = swapped(far, 1), swapped(near, 0)
        return from_far, from_near, moved(ax_minus, 0, -1), moved(ax_plus, 0, 1), ax_minus

    def step(stage, field, halos, more, more_specs):
        outs = [field_like]
        if stage < 2:
            outs += [
                f32(whole + devs, radial),
                f32(whole + devs, radial),
                f32(5 * devs, radial),
                f32(4 * devs, radial),
                f32(4 * devs, radial),
            ]
        else:
            outs += [field_like]
        if stage == 0:
            outs += [field_like, f32(2 * devs, cells_ax, radial), f32(4 * devs, radial)]
        return pl.pallas_call(
            functools.partial(step_kernel, stage, per),
            out_shape=outs,
            in_specs=[VMEM] * 10 + more_specs,
            out_specs=[VMEM if stage < 2 else HBM] * len(outs),
            scratch_shapes=[
                pltpu.VMEM((4 * devs, radial), jnp.float32),
                pltpu.VMEM((2 * devs, radial), jnp.float32),
            ]
            + [pltpu.VMEM(start_field.shape, jnp.float32), pltpu.SemaphoreType.DMA((2,))] * (stage // 2),
            compiler_params=pltpu.CompilerParams(vmem_limit_bytes=LIMIT),
        )(field, nu, far_halo, near_halo, *halos[:2], ax_behind, *halos[2:], *more)

    middle, *rest = step(0, start_field, halos, [code, offset, table], [VMEM, SMEM, SMEM])
    packed, track0, src = rest[:4], rest[4], rest[5:]
    final, *rest = step(1, middle, exchange(*packed), [*src, track0, start_field], [VMEM] * 5)
    packed, track1 = rest[:4], rest[4]
    residual, out = step(2, final, exchange(*packed), [*src, track0, track1], [VMEM] * 5)
    return out, residual


def solution(mesh):
    placed = (
        P(None, None, "az", "ax", None),
        P(None, "az", "ax", None),
        P("az", "ax", None),
        P("az", "ax", None),
        P("az", "ax", None),
        P(None, None, "az"),
        P(),
    )
    return jax.shard_map(
        shards,
        mesh=mesh,
        in_specs=placed,
        out_specs=(P(None, None, "az", "ax", None), P(None, None, "az", "ax", None)),
        check_vma=False,
    )
```

```python
import functools

import jax
import jax.numpy as jnp
from jax import lax
from jax.experimental import pallas as pl
from jax.experimental.pallas import tpu as pltpu
from jax.sharding import PartitionSpec as P

mass_term = 1.0
cheb_centre = 8.5
cheb_halfwidth = 7.5
cheb_sigma = cheb_centre / cheb_halfwidth
rho_first = 1.0 / cheb_sigma
rho_second = 1.0 / (2.0 * cheb_sigma - rho_first)

mix_second = rho_second * rho_first
step_second = 2.0 * rho_second / cheb_halfwidth

VMEM = pl.BlockSpec(memory_space=pltpu.VMEM)
SMEM = pl.BlockSpec(memory_space=pltpu.SMEM)
HBM = pl.BlockSpec(memory_space=pltpu.HBM)
ANY = pl.BlockSpec(memory_space=pl.ANY)
MIB = 1024 * 1024
LIMIT = 16 * MIB
UNROLL = 4
LIMIT_FIRST = 63 * MIB


def moved(value, shift_az, shift_ax):
    count_az, count_ax = lax.axis_size("az"), lax.axis_size("ax")
    pairs = [
        (a * count_ax + q, (a + shift_az) % count_az * count_ax + q + shift_ax)
        for a in range(count_az)
        for q in range(count_ax)
        if 0 <= q + shift_ax < count_ax
    ]
    return lax.ppermute(value, ("az", "ax"), pairs)


def swapped(value, odd):
    count_az, count_ax = lax.axis_size("az"), lax.axis_size("ax")
    pairs = [
        (a * count_ax + q, (a + (1 if a % 2 == odd else -1)) % count_az * count_ax + q)
        for a in range(count_az)
        for q in range(count_ax)
    ]
    return lax.ppermute(value, ("az", "ax"), pairs)


def swapped_ax(value, odd):
    count = lax.axis_size("ax")
    pairs = [(q, q + (1 if q % 2 == odd else -1)) for q in range(count)]
    return lax.ppermute(value, "ax", [(q, to) for q, to in pairs if 0 <= to < count])


def by_parity(axis, body, far, near):
    parity = lax.rem(lax.axis_index(axis), 2)

    @pl.when(parity == 0)
    def _():
        body(near, far)

    @pl.when(parity == 1)
    def _():
        body(far, near)


def lanes(shape):
    return lax.broadcasted_iota(jnp.int32, shape, 1)


def rows(shape):
    return lax.broadcasted_iota(jnp.int32, shape, 0)


def radial_next(v):
    tile = 128
    rolled = [pltpu.roll(v[:, at : at + tile], tile - 1, 1) for at in range(0, v.shape[1], tile)]
    last = lanes(rolled[0].shape) == tile - 1
    rolled.append(jnp.zeros_like(rolled[0]))
    return jnp.concatenate(
        [jnp.where(last, later, part) for part, later in zip(rolled, rolled[1:])], axis=1
    )


def radial_prev(v):
    tile = 128
    rolled = [pltpu.roll(v[:, at : at + tile], 1, 1) for at in range(0, v.shape[1], tile)]
    first = lanes(rolled[0].shape) == 0
    rolled.insert(0, jnp.zeros_like(rolled[0]))
    return jnp.concatenate(
        [jnp.where(first, sooner, part) for sooner, part in zip(rolled, rolled[1:])], axis=1
    )


def axial_next(v, row):
    n = v.shape[0]
    return jnp.where(rows(v.shape) == n - 1, row, pltpu.roll(v, n - 1, 0))


def axial_prev(v, row):
    return jnp.where(rows(v.shape) == 0, row, pltpu.roll(v, 1, 0))


def block(k, height):
    return pl.ds(pl.multiple_of(k * height, height), height)


def pack_az(d, height, a, minus, plus):
    minus[block(2 * d, height)] = a[1][0]
    minus[block(2 * d + 1, height)] = a[2][0]
    plus[block(2 * d, height)] = radial_next(a[0][1]) - a[0][1] + a[2][1]
    plus[block(2 * d + 1, height)] = a[0][1] - axial_next(a[0][1], 0.0) - a[1][1]


def pack_ax(d, devs, a, ax_minus, ax_plus):
    top = a[0][0].shape[0] - 1
    for i in range(2):
        ax_minus[pl.ds(i * devs + d, 1)] = a[0][i][0:1]
        ax_minus[pl.ds((2 + i) * devs + d, 1)] = a[2][i][0:1]
        end = a[1][i][top:]
        ax_plus[pl.ds(i * devs + d, 1)] = end - radial_next(end) - a[2][i][top:]
    ax_plus[pl.ds(2 * devs + d, 1)] = a[1][1][top:] - a[1][0][top:] + a[0][0][top:]
    ax_plus[pl.ds(3 * devs + d, 1)] = a[0][1][top:] - a[1][1][top:]


def edge_kernel(
    per, a_hbm, reluct_hbm, lam_hbm, mag_hbm, reg_hbm, slots_hbm,
    ax_far, ax_near, nu_ref, code_ref, offset_ref, static_ref,
    first_ref, last_ref, lam_ref, mag_ref, reg_ref, slots_ref, sems,
):
    devs = a_hbm.shape[0]
    top = nu_ref.shape[2] - 1
    copies = [
        pltpu.make_async_copy(reluct_hbm, nu_ref, sems.at[0]),
        pltpu.make_async_copy(lam_hbm, lam_ref, sems.at[1]),
        pltpu.make_async_copy(mag_hbm, mag_ref, sems.at[2]),
        pltpu.make_async_copy(reg_hbm, reg_ref, sems.at[3]),
        pltpu.make_async_copy(slots_hbm, slots_ref, sems.at[4]),
    ]
    row_copies = []
    for c in range(3):
        for i in range(2):
            to = first_ref.at[pl.ds((2 * c + i) * devs, devs)]
            if c != 1:
                row_copies.append((a_hbm.at[:, c, i, 0], to))
            to = last_ref.at[pl.ds((2 * c + i) * devs, devs)]
            row_copies.append((a_hbm.at[:, c, i, top], to))
    for k, (source, to) in enumerate(row_copies):
        copies.append(pltpu.make_async_copy(source, to, sems.at[5 + k]))
    for copy in copies:
        copy.start()
    for copy in copies[:5]:
        copy.wait()

    base = lax.axis_index("az") * per
    slots = slots_ref[...]
    count = slots.shape[1]
    slots = pltpu.roll(slots, lax.rem(2 * count - base + per, count), 1)
    row = lax.div(slots, jnp.int32(per))
    offset_ref[...] = row * (3 * devs * per) + (slots - row * per)
    for i in range(2):
        nu_ref[1, i] = nu_ref[1, i] * (1.0 + 3.0 * lam_ref[i].astype(jnp.float32))
        code_ref[i] = jnp.where(mag_ref[i] == 1, reg_ref[i] - base, -1).astype(jnp.float32)
    height = top + 1
    static_ref[pl.ds(0, height)] = nu_ref[1, 1]
    static_ref[pl.ds(height, height)] = nu_ref[2, 1]
    static_ref[pl.ds(2 * height, height)] = code_ref[1]
    for copy in copies[5:]:
        copy.wait()

    def body(ax_plus, ax_minus):
        for i in range(2):
            at = 5 * devs + i
            ax_plus[pl.ds(at, 1)] = nu_ref[0, i, top:]
            ax_plus[pl.ds(at + 2, 1)] = nu_ref[2, i, top:]
            ax_plus[pl.ds(at + 4, 1)] = code_ref[i, top:]
            ax_plus[pl.ds(at + 6, 1)] = jnp.zeros_like(code_ref[i, top:])

        firsts = [first_ref[pl.ds(k * devs, devs)] for k in (0, 1, 4, 5)]
        lasts = [[last_ref[pl.ds((2 * c + i) * devs, devs)] for i in range(2)] for c in range(3)]
        for k, first in enumerate(firsts):
            ax_minus[pl.ds(k * devs, devs)] = first
        for i in range(2):
            ax_plus[pl.ds(i * devs, devs)] = lasts[1][i] - radial_next(lasts[1][i]) - lasts[2][i]
        ax_plus[pl.ds(2 * devs, devs)] = lasts[1][1] - lasts[1][0] + lasts[0][0]
        ax_plus[pl.ds(3 * devs, devs)] = lasts[0][1] - lasts[1][1]
        ax_plus[pl.ds(4 * devs, devs)] = lasts[1][0]

    by_parity("ax", body, ax_far, ax_near)


def plane_kernel(a_ref, static_ref, far, near):
    devs, height = a_ref.shape[0], a_ref.shape[3]

    def body(plus, minus):
        plus[pl.ds(2 * devs * height + devs, 3 * height)] = static_ref[...]

        @pl.loop(0, devs, unroll=UNROLL)
        def _(d):
            a = [[a_ref[d, c, i] for i in range(2)] for c in range(3)]
            pack_az(d, height, a, minus, plus)

    by_parity("az", body, far, near)


def corner_kernel(end, devs, ax_far, ax_near, far_in, near_in, far, near, sems):
    at = pl.ds(end, devs)

    def body_ax(ax_ahead, ax_behind):
        def body(plus, minus):
            copies = [
                (ax_behind.at[pl.ds(4 * devs, devs)], minus.at[at]),
                (ax_ahead.at[pl.ds(devs, devs)], plus.at[at]),
            ]
            copies = [
                pltpu.make_async_copy(source, to, sems.at[k]) for k, (source, to) in enumerate(copies)
            ]
            for copy in copies:
                copy.start()
            for copy in copies:
                copy.wait()

        by_parity("az", body, far, near)

    by_parity("ax", body_ax, ax_far, ax_near)


def settle_kernel(halo_far, halo_near, a_ref, ahead, behind, minus):
    devs = a_ref.shape[0]

    def body(ahead_ref, behind_ref):
        ahead[...] = ahead_ref[pl.ds(0, ahead.shape[0])]
        behind[...] = behind_ref[...]

    by_parity("ax", body, halo_far, halo_near)
    for d in range(devs):
        for i in range(2):
            minus[i * devs + d : i * devs + d + 1] = a_ref[d, 0, i, 0:1]
            minus[(2 + i) * devs + d : (2 + i) * devs + d + 1] = a_ref[d, 2, i, 0:1]


def picked(nu, code, values):
    rest, weight = code, 1
    while weight < len(values):
        weight *= 2
    values = list(values) + [values[-1]] * (weight - len(values))
    while len(values) > 1:
        weight //= 2
        high = rest > weight - 0.5
        rest = jnp.where(high, rest - weight, rest)
        half = len(values) // 2
        values = [jnp.where(high, b, a) for a, b in zip(values[:half], values[half:])]
    return jnp.where(code > -0.5, nu * values[0], 0.0)


def advanced(stage, value, start, curl):
    if stage == 0:
        return value * (1.0 - mass_term / cheb_centre) - curl * (1.0 / cheb_centre)
    if stage == 1:
        return (
            value * (1.0 + mix_second - mass_term * step_second) - start * mix_second - curl * step_second
        )
    return -curl - mass_term * value


def step_kernel(stage, per, *refs):
    refs = list(refs)
    halo = [refs.pop(4), refs.pop(4)]
    statics = refs.pop(2), refs.pop(2)
    sent = [None, None]
    if stage < 2:
        first = (10, 12)[stage]
        sent = [refs.pop(first), refs.pop(first)]

    def body(plus, minus):
        step_body(stage, per, refs, plus, minus)

    by_parity("az", body, (halo[0], statics[0], sent[0]), (halo[1], statics[1], sent[1]))


def step_body(stage, per, refs, beyond_refs, behind_refs):
    it = iter(refs)
    ahead, _, plus = beyond_refs
    behind, nu_az_ref, minus = behind_refs
    a_ref, nu_ref, nu_ax_ref = next(it), next(it), next(it)
    ax_ahead, ax_behind, mine = [next(it) for _ in range(3)]
    if stage == 0:
        code_ref, offset_ref, table_ref = next(it), next(it), next(it)
    else:
        src_ref, src_az_ref, src_ax_ref, track0 = [next(it) for _ in range(4)]
    track = track0 if stage == 1 else None
    if stage == 1:
        start_ref = next(it)
    if stage == 2:
        track = next(it)
    out_ref = next(it)
    if stage < 2:
        ax_minus, ax_plus, next_track = [next(it) for _ in range(3)]
    if stage == 0:
        src_ref, src_az_ref, src_ax_ref = next(it), next(it), next(it)
    if stage == 2:
        final_hbm = next(it)
    edge, corner = next(it), next(it)
    if stage == 2:
        res_hbm, out_ref, sems = out_ref, next(it), next(it)
        leave = pltpu.make_async_copy(a_ref, final_hbm, sems.at[0])
        leave.start()
    devs, height = a_ref.shape[0], a_ref.shape[3]
    top = height - 1
    end = 2 * devs * height
    nu_az = end + devs
    nu_ax = 5 * devs
    every = pl.ds(0, devs)
    after = pl.ds(devs, devs)

    if stage == 0:
        corner[every] = behind[pl.ds(end, devs)]
        corner[after] = ahead[pl.ds(end, devs)]
    else:
        curl = ax_ahead[pl.ds(4 * devs, devs)] - track[pl.ds(2 * devs, devs)]
        value = advanced(stage - 1, track[every], track0[every], curl)
        open_end = lax.axis_index("ax") == lax.axis_size("ax") - 1
        corner[every] = jnp.where(open_end, 0.0, value)
        curl = ahead[pl.ds(end, devs)] + track[pl.ds(3 * devs, devs)]
        corner[after] = advanced(stage - 1, track[after], track0[after], curl)

    def values(d, c, first):
        return [
            table_ref[offset_ref[d, first + k] + (c * devs + d) * per] for k in range(per)
        ]

    if stage == 0:

        @pl.loop(0, devs, unroll=UNROLL)
        def _(d):
            for c in (0, 2):
                own = values(d, c, per)
                for i in range(2):
                    src_ax_ref[pl.ds((c + i) * devs + d, 1)] = picked(
                        nu_ax_ref[pl.ds(nu_ax + c + i, 1)], nu_ax_ref[pl.ds(nu_ax + 4 + i, 1)], own
                    )

    for at, own, sign in ((0, 2, 1.0), (1, 3, 1.0), (2, 0, -1.0), (3, 1, -1.0)):
        part = pl.ds(at * devs, devs)
        flux = ax_behind[part] + sign * mine[pl.ds(own * devs, devs)]
        if at == 3:
            flux = flux + corner[after]
        edge[part] = nu_ax_ref[pl.ds(nu_ax + at, 1)] * flux - src_ax_ref[part]
    if stage < 2:
        before = edge[every]
        minus[pl.ds(end, devs)] = before - radial_prev(before) - edge[pl.ds(2 * devs, devs)]
        next_track[pl.ds(0, 2 * devs)] = corner[...]
        next_track[pl.ds(3 * devs, devs)] = edge[pl.ds(3 * devs, devs)]

    @pl.loop(0, devs, unroll=UNROLL)
    def _(d):
        a = [[a_ref[d, c, i] for i in range(2)] for c in range(3)]
        up = [None, ahead[block(2 * d, height)], ahead[block(2 * d + 1, height)]]
        inten = [[None, None], [None, None], [None, None]]
        own = [values(d, c, per) for c in range(3)] if stage == 0 else None
        for i in range(2):
            next1 = a[1][1] if i == 0 else up[1]
            next2 = a[2][1] if i == 0 else up[2]
            row0 = ax_ahead[pl.ds(i * devs + d, 1)]
            row2 = ax_ahead[pl.ds((2 + i) * devs + d, 1)]
            flux = (
                (axial_next(a[2][i], row2) - a[2][i]) - (radial_next(a[1][i]) - a[1][i]),
                (radial_next(a[0][i]) - a[0][i]) - (next2 - a[2][i]),
                (next1 - a[1][i]) - (axial_next(a[0][i], row0) - a[0][i]),
            )
            for c in range(3):
                if stage == 0:
                    src = picked(nu_ref[c, i], code_ref[i], own[c])
                    src_ref[d, c, i] = src
                else:
                    src = src_ref[d, c, i]
                inten[c][i] = nu_ref[c, i] * flux[c] - src
        back_src = [None, None]
        for c in range(1, 3):
            if stage == 0:
                src = picked(
                    nu_az_ref[pl.ds(nu_az + (c - 1) * height, height)],
                    nu_az_ref[pl.ds(nu_az + 2 * height, height)],
                    values(d, c, 0),
                )
                src_az_ref[2 * d + c - 1] = src
            else:
                src = src_az_ref[2 * d + c - 1]
            back_src[c - 1] = src
        beyond = jnp.where(rows(a[1][0].shape) == top, corner[pl.ds(d, 1)], 0.0)
        back1 = nu_az_ref[pl.ds(nu_az, height)] * (behind[block(2 * d, height)] - a[2][0]) - back_src[0]
        back2 = (
            nu_az_ref[pl.ds(nu_az + height, height)]
            * (behind[block(2 * d + 1, height)] + a[1][0] - beyond)
            - back_src[1]
        )
        new = [[None, None], [None, None], [None, None]]
        for i in range(2):
            prev1 = back1 if i == 0 else inten[1][0]
            prev2 = back2 if i == 0 else inten[2][0]
            row0 = edge[pl.ds(i * devs + d, 1)]
            row2 = edge[pl.ds((2 + i) * devs + d, 1)]
            i0, i1, i2 = inten[0][i], inten[1][i], inten[2][i]
            curl = (
                (i2 - axial_prev(i2, row2)) - (i1 - radial_prev(i1)),
                (i0 - radial_prev(i0)) - (i2 - prev2),
                (i1 - prev1) - (i0 - axial_prev(i0, row0)),
            )
            for c in range(3):
                start = start_ref[d, c, i] if stage == 1 else None
                value = advanced(stage, a[c][i], start, curl[c])
                out_ref[d, c, i] = value
                new[c][i] = value
        if stage == 2:
            pltpu.make_async_copy(out_ref.at[d], res_hbm.at[d], sems.at[1]).start()
        if stage < 2:
            first1, first2 = back1[0:1], back2[0:1]
            ax_minus[pl.ds(4 * devs + d, 1)] = first2 - (first1 - radial_prev(first1))
            next_track[pl.ds(2 * devs + d, 1)] = back2[top:]
            pack_az(d, height, new, minus, plus)
            pack_ax(d, devs, new, ax_minus, ax_plus)

    if stage == 2:
        leave.wait()
        pltpu.make_async_copy(out_ref, res_hbm, sems.at[1]).wait()


def f32(*shape):
    return jax.ShapeDtypeStruct(shape, jnp.float32)


def shards(start_field, reluctivity, lamination, magnets, region_ids, pieces, slot_map):
    devs, comps, cells_az, cells_ax, radial = start_field.shape
    count_az = lax.axis_size("az")
    per = pieces.shape[2]
    whole = 2 * devs * cells_ax

    field_like = f32(*start_field.shape)
    edges = [
        f32(5 * devs + 8, radial),
        f32(5 * devs + 8, radial),
        f32(*reluctivity.shape),
        f32(*lamination.shape),
        jax.ShapeDtypeStruct(slot_map.shape, jnp.int32),
        f32(3 * cells_ax, radial),
    ]
    ax_far, ax_near, nu, code, offset, static = pl.pallas_call(
        functools.partial(edge_kernel, per),
        out_shape=edges,
        in_specs=[HBM] * 6,
        out_specs=[VMEM] * len(edges),
        scratch_shapes=[pltpu.VMEM((6 * devs, radial), jnp.float32)] * 2
        + [pltpu.VMEM(lamination.shape, jnp.int32)] * 3
        + [pltpu.VMEM(slot_map.shape, jnp.int32), pltpu.SemaphoreType.DMA((15,))],
        compiler_params=pltpu.CompilerParams(vmem_limit_bytes=LIMIT_FIRST),
    )(start_field, reluctivity, lamination, magnets, region_ids, slot_map)
    ax_halos = swapped_ax(ax_far, 1), swapped_ax(ax_near, 0)
    planes = [f32(whole + devs + 3 * cells_ax, radial)] * 2
    packed = pl.pallas_call(
        plane_kernel,
        out_shape=planes,
        in_specs=[VMEM] * 2,
        out_specs=[VMEM] * 2,
        compiler_params=pltpu.CompilerParams(vmem_limit_bytes=LIMIT),
        cost_estimate=pl.CostEstimate(flops=10**7, bytes_accessed=3 * MIB, transcendentals=0),
    )(start_field, static)
    far, near = pl.pallas_call(
        functools.partial(corner_kernel, whole, devs),
        out_shape=planes,
        in_specs=[VMEM, VMEM, ANY, ANY],
        out_specs=[ANY] * 2,
        scratch_shapes=[pltpu.SemaphoreType.DMA((2,))],
        input_output_aliases={2: 0, 3: 1},
        compiler_params=pltpu.CompilerParams(vmem_limit_bytes=LIMIT),
    )(*ax_halos, *packed)
    ax_ahead, ax_behind, ax_minus = pl.pallas_call(
        settle_kernel,
        out_shape=[f32(4 * devs, radial), f32(5 * devs + 8, radial), f32(4 * devs, radial)],
        in_specs=[VMEM] * 3,
        out_specs=[VMEM] * 3,
        compiler_params=pltpu.CompilerParams(vmem_limit_bytes=LIMIT),
    )(*ax_halos, start_field)
    far_halo, near_halo = swapped(far, 1), swapped(near, 0)
    halos = (far_halo, near_halo, ax_ahead, ax_behind, ax_minus)
    flat = pieces.reshape(1, comps * devs * per)
    table = lax.all_to_all(
        jnp.broadcast_to(flat, (count_az, comps * devs * per)), "az", 0, 0, tiled=True
    ).reshape(-1)

    def exchange(far, near, ax_minus, ax_plus):
        from_far, from_near = swapped(far, 1), swapped(near, 0)
        return from_far, from_near, moved(ax_minus, 0, -1), moved(ax_plus, 0, 1), ax_minus

    def step(stage, field, halos, more, more_specs):
        outs = [field_like]
        if stage < 2:
            outs += [
                f32(whole + devs, radial),
                f32(whole + devs, radial),
                f32(5 * devs, radial),
                f32(4 * devs, radial),
                f32(4 * devs, radial),
            ]
        else:
            outs += [field_like]
        if stage == 0:
            outs += [field_like, f32(2 * devs, cells_ax, radial), f32(4 * devs, radial)]
        return pl.pallas_call(
            functools.partial(step_kernel, stage, per),
            out_shape=outs,
            in_specs=[VMEM] * 10 + more_specs,
            out_specs=[VMEM if stage < 2 else HBM] * len(outs),
            scratch_shapes=[
                pltpu.VMEM((4 * devs, radial), jnp.float32),
                pltpu.VMEM((2 * devs, radial), jnp.float32),
            ]
            + [pltpu.VMEM(start_field.shape, jnp.float32), pltpu.SemaphoreType.DMA((2,))] * (stage // 2),
            compiler_params=pltpu.CompilerParams(vmem_limit_bytes=LIMIT),
        )(field, nu, far_halo, near_halo, *halos[:2], ax_behind, *halos[2:], *more)

    middle, *rest = step(0, start_field, halos, [code, offset, table], [VMEM, SMEM, SMEM])
    packed, track0, src = rest[:4], rest[4], rest[5:]
    final, *rest = step(1, middle, exchange(*packed), [*src, track0, start_field], [VMEM] * 5)
    packed, track1 = rest[:4], rest[4]
    residual, out = step(2, final, exchange(*packed), [*src, track0, track1], [VMEM] * 5)
    return out, residual


def solution(mesh):
    placed = (
        P(None, None, "az", "ax", None),
        P(None, "az", "ax", None),
        P("az", "ax", None),
        P("az", "ax", None),
        P("az", "ax", None),
        P(None, None, "az"),
        P(),
    )
    return jax.shard_map(
        shards,
        mesh=mesh,
        in_specs=placed,
        out_specs=(P(None, None, "az", "ax", None), P(None, None, "az", "ax", None)),
        check_vma=False,
    )
```

```python
import functools

import jax
import jax.numpy as jnp
from jax import lax
from jax.experimental import pallas as pl
from jax.experimental.pallas import tpu as pltpu
from jax.sharding import PartitionSpec as P

mass_term = 1.0
cheb_centre = 8.5
cheb_halfwidth = 7.5
cheb_sigma = cheb_centre / cheb_halfwidth
rho_first = 1.0 / cheb_sigma
rho_second = 1.0 / (2.0 * cheb_sigma - rho_first)

mix_second = rho_second * rho_first
step_second = 2.0 * rho_second / cheb_halfwidth

VMEM = pl.BlockSpec(memory_space=pltpu.VMEM)
SMEM = pl.BlockSpec(memory_space=pltpu.SMEM)
HBM = pl.BlockSpec(memory_space=pltpu.HBM)
ANY = pl.BlockSpec(memory_space=pl.ANY)
MIB = 1024 * 1024
LIMIT = 16 * MIB
UNROLL = 4
LIMIT_FIRST = 63 * MIB


def moved(value, shift_az, shift_ax):
    count_az, count_ax = lax.axis_size("az"), lax.axis_size("ax")
    pairs = [
        (a * count_ax + q, (a + shift_az) % count_az * count_ax + q + shift_ax)
        for a in range(count_az)
        for q in range(count_ax)
        if 0 <= q + shift_ax < count_ax
    ]
    return lax.ppermute(value, ("az", "ax"), pairs)


def swapped(value, odd):
    count_az, count_ax = lax.axis_size("az"), lax.axis_size("ax")
    pairs = [
        (a * count_ax + q, (a + (1 if a % 2 == odd else -1)) % count_az * count_ax + q)
        for a in range(count_az)
        for q in range(count_ax)
    ]
    return lax.ppermute(value, ("az", "ax"), pairs)


def swapped_ax(value, odd):
    count = lax.axis_size("ax")
    pairs = [(q, q + (1 if q % 2 == odd else -1)) for q in range(count)]
    return lax.ppermute(value, "ax", [(q, to) for q, to in pairs if 0 <= to < count])


def by_parity(axis, body, far, near):
    parity = lax.rem(lax.axis_index(axis), 2)

    @pl.when(parity == 0)
    def _():
        body(near, far)

    @pl.when(parity == 1)
    def _():
        body(far, near)


def lanes(shape):
    return lax.broadcasted_iota(jnp.int32, shape, 1)


def rows(shape):
    return lax.broadcasted_iota(jnp.int32, shape, 0)


def radial_next(v):
    tile = 128
    rolled = [pltpu.roll(v[:, at : at + tile], tile - 1, 1) for at in range(0, v.shape[1], tile)]
    last = lanes(rolled[0].shape) == tile - 1
    rolled.append(jnp.zeros_like(rolled[0]))
    return jnp.concatenate(
        [jnp.where(last, later, part) for part, later in zip(rolled, rolled[1:])], axis=1
    )


def radial_prev(v):
    tile = 128
    rolled = [pltpu.roll(v[:, at : at + tile], 1, 1) for at in range(0, v.shape[1], tile)]
    first = lanes(rolled[0].shape) == 0
    rolled.insert(0, jnp.zeros_like(rolled[0]))
    return jnp.concatenate(
        [jnp.where(first, sooner, part) for sooner, part in zip(rolled, rolled[1:])], axis=1
    )


def axial_next(v, row):
    n = v.shape[0]
    return jnp.where(rows(v.shape) == n - 1, row, pltpu.roll(v, n - 1, 0))


def axial_prev(v, row):
    return jnp.where(rows(v.shape) == 0, row, pltpu.roll(v, 1, 0))


def block(k, height):
    return pl.ds(pl.multiple_of(k * height, height), height)


def pack_az(d, height, a, minus, plus):
    minus[block(2 * d, height)] = a[1][0]
    minus[block(2 * d + 1, height)] = a[2][0]
    plus[block(2 * d, height)] = radial_next(a[0][1]) - a[0][1] + a[2][1]
    plus[block(2 * d + 1, height)] = a[0][1] - axial_next(a[0][1], 0.0) - a[1][1]


def pack_ax(d, devs, a, ax_minus, ax_plus):
    top = a[0][0].shape[0] - 1
    for i in range(2):
        ax_minus[pl.ds(i * devs + d, 1)] = a[0][i][0:1]
        ax_minus[pl.ds((2 + i) * devs + d, 1)] = a[2][i][0:1]
        end = a[1][i][top:]
        ax_plus[pl.ds(i * devs + d, 1)] = end - radial_next(end) - a[2][i][top:]
    ax_plus[pl.ds(2 * devs + d, 1)] = a[1][1][top:] - a[1][0][top:] + a[0][0][top:]
    ax_plus[pl.ds(3 * devs + d, 1)] = a[0][1][top:] - a[1][1][top:]


def edge_kernel(
    per, a_hbm, reluct_hbm, lam_hbm, mag_hbm, reg_hbm, slots_hbm,
    ax_far, ax_near, nu_ref, code_ref, offset_ref, static_ref,
    first_ref, last_ref, lam_ref, mag_ref, reg_ref, slots_ref, sems,
):
    devs = a_hbm.shape[0]
    top = nu_ref.shape[2] - 1
    copies = [
        pltpu.make_async_copy(reluct_hbm, nu_ref, sems.at[0]),
        pltpu.make_async_copy(lam_hbm, lam_ref, sems.at[1]),
        pltpu.make_async_copy(mag_hbm, mag_ref, sems.at[2]),
        pltpu.make_async_copy(reg_hbm, reg_ref, sems.at[3]),
        pltpu.make_async_copy(slots_hbm, slots_ref, sems.at[4]),
    ]
    row_copies = []
    for c in range(3):
        for i in range(2):
            to = first_ref.at[pl.ds((2 * c + i) * devs, devs)]
            if c != 1:
                row_copies.append((a_hbm.at[:, c, i, 0], to))
            to = last_ref.at[pl.ds((2 * c + i) * devs, devs)]
            row_copies.append((a_hbm.at[:, c, i, top], to))
    for k, (source, to) in enumerate(row_copies):
        copies.append(pltpu.make_async_copy(source, to, sems.at[5 + k]))
    for copy in copies:
        copy.start()
    for copy in copies[:5]:
        copy.wait()

    base = lax.axis_index("az") * per
    slots = slots_ref[...]
    count = slots.shape[1]
    slots = pltpu.roll(slots, lax.rem(2 * count - base + per, count), 1)
    row = lax.div(slots, jnp.int32(per))
    offset_ref[...] = row * (3 * devs * per) + (slots - row * per)
    for i in range(2):
        nu_ref[1, i] = nu_ref[1, i] * (1.0 + 3.0 * lam_ref[i].astype(jnp.float32))
        code_ref[i] = jnp.where(mag_ref[i] == 1, reg_ref[i] - base, -1).astype(jnp.float32)
    height = top + 1
    static_ref[pl.ds(0, height)] = nu_ref[1, 1]
    static_ref[pl.ds(height, height)] = nu_ref[2, 1]
    static_ref[pl.ds(2 * height, height)] = code_ref[1]
    for copy in copies[5:]:
        copy.wait()

    def body(ax_plus, ax_minus):
        for i in range(2):
            at = 5 * devs + i
            ax_plus[pl.ds(at, 1)] = nu_ref[0, i, top:]
            ax_plus[pl.ds(at + 2, 1)] = nu_ref[2, i, top:]
            ax_plus[pl.ds(at + 4, 1)] = code_ref[i, top:]
            ax_plus[pl.ds(at + 6, 1)] = jnp.zeros_like(code_ref[i, top:])

        firsts = [first_ref[pl.ds(k * devs, devs)] for k in (0, 1, 4, 5)]
        lasts = [[last_ref[pl.ds((2 * c + i) * devs, devs)] for i in range(2)] for c in range(3)]
        for k, first in enumerate(firsts):
            ax_minus[pl.ds(k * devs, devs)] = first
        for i in range(2):
            ax_plus[pl.ds(i * devs, devs)] = lasts[1][i] - radial_next(lasts[1][i]) - lasts[2][i]
        ax_plus[pl.ds(2 * devs, devs)] = lasts[1][1] - lasts[1][0] + lasts[0][0]
        ax_plus[pl.ds(3 * devs, devs)] = lasts[0][1] - lasts[1][1]
        ax_plus[pl.ds(4 * devs, devs)] = lasts[1][0]

    by_parity("ax", body, ax_far, ax_near)


def plane_kernel(a_ref, static_ref, far, near):
    devs, height = a_ref.shape[0], a_ref.shape[3]

    def body(plus, minus):
        plus[pl.ds(2 * devs * height + devs, 3 * height)] = static_ref[...]

        @pl.loop(0, devs, unroll=UNROLL)
        def _(d):
            a = [[a_ref[d, c, i] for i in range(2)] for c in range(3)]
            pack_az(d, height, a, minus, plus)

    by_parity("az", body, far, near)


def corner_kernel(end, devs, ax_far, ax_near, far_in, near_in, far, near, sems):
    at = pl.ds(end, devs)

    def body_ax(ax_ahead, ax_behind):
        def body(plus, minus):
            copies = [
                (ax_behind.at[pl.ds(4 * devs, devs)], minus.at[at]),
                (ax_ahead.at[pl.ds(devs, devs)], plus.at[at]),
            ]
            copies = [
                pltpu.make_async_copy(source, to, sems.at[k]) for k, (source, to) in enumerate(copies)
            ]
            for copy in copies:
                copy.start()
            for copy in copies:
                copy.wait()

        by_parity("az", body, far, near)

    by_parity("ax", body_ax, ax_far, ax_near)


def settle_kernel(halo_far, halo_near, a_ref, ahead, behind, minus):
    devs = a_ref.shape[0]

    def body(ahead_ref, behind_ref):
        ahead[...] = ahead_ref[pl.ds(0, ahead.shape[0])]
        behind[...] = behind_ref[...]

    by_parity("ax", body, halo_far, halo_near)
    for d in range(devs):
        for i in range(2):
            minus[i * devs + d : i * devs + d + 1] = a_ref[d, 0, i, 0:1]
            minus[(2 + i) * devs + d : (2 + i) * devs + d + 1] = a_ref[d, 2, i, 0:1]


def picked(nu, code, values):
    rest, weight = code, 1
    while weight < len(values):
        weight *= 2
    values = list(values) + [values[-1]] * (weight - len(values))
    while len(values) > 1:
        weight //= 2
        high = rest > weight - 0.5
        rest = jnp.where(high, rest - weight, rest)
        half = len(values) // 2
        values = [jnp.where(high, b, a) for a, b in zip(values[:half], values[half:])]
    return jnp.where(code > -0.5, nu * values[0], 0.0)


def advanced(stage, value, start, curl):
    if stage == 0:
        return value * (1.0 - mass_term / cheb_centre) - curl * (1.0 / cheb_centre)
    if stage == 1:
        return (
            value * (1.0 + mix_second - mass_term * step_second) - start * mix_second - curl * step_second
        )
    return -curl - mass_term * value


def flux_of(d, devs, a, up1, up2, ax_ahead):
    flux = [[None, None], [None, None], [None, None]]
    for i in range(2):
        next1 = a[1][1] if i == 0 else up1
        next2 = a[2][1] if i == 0 else up2
        row0 = ax_ahead[pl.ds(i * devs + d, 1)]
        row2 = ax_ahead[pl.ds((2 + i) * devs + d, 1)]
        flux[0][i] = (axial_next(a[2][i], row2) - a[2][i]) - (radial_next(a[1][i]) - a[1][i])
        flux[1][i] = (radial_next(a[0][i]) - a[0][i]) - (next2 - a[2][i])
        flux[2][i] = (next1 - a[1][i]) - (axial_next(a[0][i], row0) - a[0][i])
    return flux


def flux_kernel(a_ref, nu_ref, src_ref, ax_ahead, out_ref):
    devs = a_ref.shape[0]

    @pl.loop(0, devs, unroll=UNROLL)
    def _(d):
        a = [[a_ref[d, c, i] for i in range(2)] for c in range(3)]
        flux = flux_of(d, devs, a, 0.0, 0.0, ax_ahead)
        for c in range(3):
            for i in range(2):
                out_ref[d, c, i] = nu_ref[c, i] * flux[c][i] - src_ref[d, c, i]


def step_kernel(stage, per, *refs):
    refs = list(refs)
    halo = [refs.pop(4), refs.pop(4)]
    statics = refs.pop(2), refs.pop(2)
    sent = [None, None]
    if stage < 2:
        first = (10, 12)[stage]
        sent = [refs.pop(first), refs.pop(first)]

    def body(plus, minus):
        step_body(stage, per, refs, plus, minus)

    by_parity("az", body, (halo[0], statics[0], sent[0]), (halo[1], statics[1], sent[1]))


def step_body(stage, per, refs, beyond_refs, behind_refs):
    it = iter(refs)
    ahead, _, plus = beyond_refs
    behind, nu_az_ref, minus = behind_refs
    a_ref, nu_ref, nu_ax_ref = next(it), next(it), next(it)
    ax_ahead, ax_behind, mine = [next(it) for _ in range(3)]
    if stage == 0:
        code_ref, offset_ref, table_ref = next(it), next(it), next(it)
    else:
        src_ref, src_az_ref, src_ax_ref, track0 = [next(it) for _ in range(4)]
    track = track0 if stage == 1 else None
    if stage == 1:
        start_ref = next(it)
    if stage == 2:
        track = next(it)
    out_ref = next(it)
    if stage < 2:
        ax_minus, ax_plus, next_track = [next(it) for _ in range(3)]
    if stage == 0:
        src_ref, src_az_ref, src_ax_ref = next(it), next(it), next(it)
    if stage == 2:
        final_hbm = next(it)
    edge, corner = next(it), next(it)
    if stage == 2:
        res_hbm, out_ref, sems = out_ref, next(it), next(it)
        leave = pltpu.make_async_copy(a_ref, final_hbm, sems.at[0])
        leave.start()
    devs, height = a_ref.shape[0], a_ref.shape[3]
    top = height - 1
    end = 2 * devs * height
    nu_az = end + devs
    nu_ax = 5 * devs
    every = pl.ds(0, devs)
    after = pl.ds(devs, devs)

    if stage == 0:
        corner[every] = behind[pl.ds(end, devs)]
        corner[after] = ahead[pl.ds(end, devs)]
    else:
        curl = ax_ahead[pl.ds(4 * devs, devs)] - track[pl.ds(2 * devs, devs)]
        value = advanced(stage - 1, track[every], track0[every], curl)
        open_end = lax.axis_index("ax") == lax.axis_size("ax") - 1
        corner[every] = jnp.where(open_end, 0.0, value)
        curl = ahead[pl.ds(end, devs)] + track[pl.ds(3 * devs, devs)]
        corner[after] = advanced(stage - 1, track[after], track0[after], curl)

    def values(d, c, first):
        return [
            table_ref[offset_ref[d, first + k] + (c * devs + d) * per] for k in range(per)
        ]

    if stage == 0:

        @pl.loop(0, devs, unroll=UNROLL)
        def _(d):
            for c in (0, 2):
                own = values(d, c, per)
                for i in range(2):
                    src_ax_ref[pl.ds((c + i) * devs + d, 1)] = picked(
                        nu_ax_ref[pl.ds(nu_ax + c + i, 1)], nu_ax_ref[pl.ds(nu_ax + 4 + i, 1)], own
                    )

    for at, own, sign in ((0, 2, 1.0), (1, 3, 1.0), (2, 0, -1.0), (3, 1, -1.0)):
        part = pl.ds(at * devs, devs)
        flux = ax_behind[part] + sign * mine[pl.ds(own * devs, devs)]
        if at == 3:
            flux = flux + corner[after]
        edge[part] = nu_ax_ref[pl.ds(nu_ax + at, 1)] * flux - src_ax_ref[part]
    if stage < 2:
        before = edge[every]
        minus[pl.ds(end, devs)] = before - radial_prev(before) - edge[pl.ds(2 * devs, devs)]
        next_track[pl.ds(0, 2 * devs)] = corner[...]
        next_track[pl.ds(3 * devs, devs)] = edge[pl.ds(3 * devs, devs)]

    @pl.loop(0, devs, unroll=UNROLL)
    def _(d):
        a = [[a_ref[d, c, i] for i in range(2)] for c in range(3)]
        up = [None, ahead[block(2 * d, height)], ahead[block(2 * d + 1, height)]]
        inten = [[None, None], [None, None], [None, None]]
        own = [values(d, c, per) for c in range(3)] if stage == 0 else None
        if stage == 0:
            fluxes = flux_of(d, devs, a, up[1], up[2], ax_ahead)
        for i in range(2):
            for c in range(3):
                if stage == 0:
                    src = picked(nu_ref[c, i], code_ref[i], own[c])
                    src_ref[d, c, i] = src
                    inten[c][i] = nu_ref[c, i] * fluxes[c][i] - src
                else:
                    inten[c][i] = src_ref[d, c, i]
        if stage > 0:
            inten[1][1] = inten[1][1] - nu_ref[1, 1] * up[2]
            inten[2][1] = inten[2][1] + nu_ref[2, 1] * up[1]
        back_src = [None, None]
        for c in range(1, 3):
            if stage == 0:
                src = picked(
                    nu_az_ref[pl.ds(nu_az + (c - 1) * height, height)],
                    nu_az_ref[pl.ds(nu_az + 2 * height, height)],
                    values(d, c, 0),
                )
                src_az_ref[2 * d + c - 1] = src
            else:
                src = src_az_ref[2 * d + c - 1]
            back_src[c - 1] = src
        beyond = jnp.where(rows(a[1][0].shape) == top, corner[pl.ds(d, 1)], 0.0)
        back1 = nu_az_ref[pl.ds(nu_az, height)] * (behind[block(2 * d, height)] - a[2][0]) - back_src[0]
        back2 = (
            nu_az_ref[pl.ds(nu_az + height, height)]
            * (behind[block(2 * d + 1, height)] + a[1][0] - beyond)
            - back_src[1]
        )
        new = [[None, None], [None, None], [None, None]]
        for i in range(2):
            prev1 = back1 if i == 0 else inten[1][0]
            prev2 = back2 if i == 0 else inten[2][0]
            row0 = edge[pl.ds(i * devs + d, 1)]
            row2 = edge[pl.ds((2 + i) * devs + d, 1)]
            i0, i1, i2 = inten[0][i], inten[1][i], inten[2][i]
            curl = (
                (i2 - axial_prev(i2, row2)) - (i1 - radial_prev(i1)),
                (i0 - radial_prev(i0)) - (i2 - prev2),
                (i1 - prev1) - (i0 - axial_prev(i0, row0)),
            )
            for c in range(3):
                start = start_ref[d, c, i] if stage == 1 else None
                value = advanced(stage, a[c][i], start, curl[c])
                out_ref[d, c, i] = value
                new[c][i] = value
        if stage == 2:
            pltpu.make_async_copy(out_ref.at[d], res_hbm.at[d], sems.at[1]).start()
        if stage < 2:
            first1, first2 = back1[0:1], back2[0:1]
            ax_minus[pl.ds(4 * devs + d, 1)] = first2 - (first1 - radial_prev(first1))
            next_track[pl.ds(2 * devs + d, 1)] = back2[top:]
            pack_az(d, height, new, minus, plus)
            pack_ax(d, devs, new, ax_minus, ax_plus)

    if stage == 2:
        leave.wait()
        pltpu.make_async_copy(out_ref, res_hbm, sems.at[1]).wait()


def f32(*shape):
    return jax.ShapeDtypeStruct(shape, jnp.float32)


def shards(start_field, reluctivity, lamination, magnets, region_ids, pieces, slot_map):
    devs, comps, cells_az, cells_ax, radial = start_field.shape
    count_az = lax.axis_size("az")
    per = pieces.shape[2]
    whole = 2 * devs * cells_ax

    field_like = f32(*start_field.shape)
    edges = [
        f32(5 * devs + 8, radial),
        f32(5 * devs + 8, radial),
        f32(*reluctivity.shape),
        f32(*lamination.shape),
        jax.ShapeDtypeStruct(slot_map.shape, jnp.int32),
        f32(3 * cells_ax, radial),
    ]
    ax_far, ax_near, nu, code, offset, static = pl.pallas_call(
        functools.partial(edge_kernel, per),
        out_shape=edges,
        in_specs=[HBM] * 6,
        out_specs=[VMEM] * len(edges),
        scratch_shapes=[pltpu.VMEM((6 * devs, radial), jnp.float32)] * 2
        + [pltpu.VMEM(lamination.shape, jnp.int32)] * 3
        + [pltpu.VMEM(slot_map.shape, jnp.int32), pltpu.SemaphoreType.DMA((15,))],
        compiler_params=pltpu.CompilerParams(vmem_limit_bytes=LIMIT_FIRST),
    )(start_field, reluctivity, lamination, magnets, region_ids, slot_map)
    ax_halos = swapped_ax(ax_far, 1), swapped_ax(ax_near, 0)
    planes = [f32(whole + devs + 3 * cells_ax, radial)] * 2
    packed = pl.pallas_call(
        plane_kernel,
        out_shape=planes,
        in_specs=[VMEM] * 2,
        out_specs=[VMEM] * 2,
        compiler_params=pltpu.CompilerParams(vmem_limit_bytes=LIMIT),
        cost_estimate=pl.CostEstimate(flops=10**7, bytes_accessed=3 * MIB, transcendentals=0),
    )(start_field, static)
    far, near = pl.pallas_call(
        functools.partial(corner_kernel, whole, devs),
        out_shape=planes,
        in_specs=[VMEM, VMEM, ANY, ANY],
        out_specs=[ANY] * 2,
        scratch_shapes=[pltpu.SemaphoreType.DMA((2,))],
        input_output_aliases={2: 0, 3: 1},
        compiler_params=pltpu.CompilerParams(vmem_limit_bytes=LIMIT),
    )(*ax_halos, *packed)
    ax_ahead, ax_behind, ax_minus = pl.pallas_call(
        settle_kernel,
        out_shape=[f32(4 * devs, radial), f32(5 * devs + 8, radial), f32(4 * devs, radial)],
        in_specs=[VMEM] * 3,
        out_specs=[VMEM] * 3,
        compiler_params=pltpu.CompilerParams(vmem_limit_bytes=LIMIT),
    )(*ax_halos, start_field)
    far_halo, near_halo = swapped(far, 1), swapped(near, 0)
    halos = (far_halo, near_halo, ax_ahead, ax_behind, ax_minus)
    flat = pieces.reshape(1, comps * devs * per)
    table = lax.all_to_all(
        jnp.broadcast_to(flat, (count_az, comps * devs * per)), "az", 0, 0, tiled=True
    ).reshape(-1)

    def exchange(far, near, ax_minus, ax_plus):
        from_far, from_near = swapped(far, 1), swapped(near, 0)
        return from_far, from_near, moved(ax_minus, 0, -1), moved(ax_plus, 0, 1), ax_minus

    def step(stage, field, halos, more, more_specs):
        outs = [field_like]
        if stage < 2:
            outs += [
                f32(whole + devs, radial),
                f32(whole + devs, radial),
                f32(5 * devs, radial),
                f32(4 * devs, radial),
                f32(4 * devs, radial),
            ]
        else:
            outs += [field_like]
        if stage == 0:
            outs += [field_like, f32(2 * devs, cells_ax, radial), f32(4 * devs, radial)]
        return pl.pallas_call(
            functools.partial(step_kernel, stage, per),
            out_shape=outs,
            in_specs=[VMEM] * 10 + more_specs,
            out_specs=[VMEM if stage < 2 else HBM] * len(outs),
            scratch_shapes=[
                pltpu.VMEM((4 * devs, radial), jnp.float32),
                pltpu.VMEM((2 * devs, radial), jnp.float32),
            ]
            + [pltpu.VMEM(start_field.shape, jnp.float32), pltpu.SemaphoreType.DMA((2,))] * (stage // 2),
            compiler_params=pltpu.CompilerParams(vmem_limit_bytes=LIMIT),
        )(field, nu, far_halo, near_halo, *halos[:2], ax_behind, *halos[2:], *more)

    def known(field, halos):
        return pl.pallas_call(
            flux_kernel,
            out_shape=field_like,
            in_specs=[VMEM] * 4,
            out_specs=VMEM,
            compiler_params=pltpu.CompilerParams(vmem_limit_bytes=LIMIT),
            cost_estimate=pl.CostEstimate(flops=10**7, bytes_accessed=5 * MIB, transcendentals=0),
        )(field, nu, src[0], halos[2])

    middle, *rest = step(0, start_field, halos, [code, offset, table], [VMEM, SMEM, SMEM])
    packed, track0, src = rest[:4], rest[4], rest[5:]
    halos = exchange(*packed)
    more = [known(middle, halos), *src[1:], track0, start_field]
    final, *rest = step(1, middle, halos, more, [VMEM] * 5)
    packed, track1 = rest[:4], rest[4]
    halos = exchange(*packed)
    more = [known(final, halos), *src[1:], track0, track1]
    residual, out = step(2, final, halos, more, [VMEM] * 5)
    return out, residual


def solution(mesh):
    placed = (
        P(None, None, "az", "ax", None),
        P(None, "az", "ax", None),
        P("az", "ax", None),
        P("az", "ax", None),
        P("az", "ax", None),
        P(None, None, "az"),
        P(),
    )
    return jax.shard_map(
        shards,
        mesh=mesh,
        in_specs=placed,
        out_specs=(P(None, None, "az", "ax", None), P(None, None, "az", "ax", None)),
        check_vma=False,
    )
```

```python
import functools

import jax
import jax.numpy as jnp
from jax import lax
from jax.experimental import pallas as pl
from jax.experimental.pallas import tpu as pltpu
from jax.sharding import PartitionSpec as P

mass_term = 1.0
cheb_centre = 8.5
cheb_halfwidth = 7.5
cheb_sigma = cheb_centre / cheb_halfwidth
rho_first = 1.0 / cheb_sigma
rho_second = 1.0 / (2.0 * cheb_sigma - rho_first)

mix_second = rho_second * rho_first
step_second = 2.0 * rho_second / cheb_halfwidth

VMEM = pl.BlockSpec(memory_space=pltpu.VMEM)
SMEM = pl.BlockSpec(memory_space=pltpu.SMEM)
HBM = pl.BlockSpec(memory_space=pltpu.HBM)
ANY = pl.BlockSpec(memory_space=pl.ANY)
MIB = 1024 * 1024
LIMIT = 16 * MIB
UNROLL = 4
LIMIT_FIRST = 63 * MIB


def moved(value, shift_az, shift_ax):
    count_az, count_ax = lax.axis_size("az"), lax.axis_size("ax")
    pairs = [
        (a * count_ax + q, (a + shift_az) % count_az * count_ax + q + shift_ax)
        for a in range(count_az)
        for q in range(count_ax)
        if 0 <= q + shift_ax < count_ax
    ]
    return lax.ppermute(value, ("az", "ax"), pairs)


def swapped(value, odd):
    count_az, count_ax = lax.axis_size("az"), lax.axis_size("ax")
    pairs = [
        (a * count_ax + q, (a + (1 if a % 2 == odd else -1)) % count_az * count_ax + q)
        for a in range(count_az)
        for q in range(count_ax)
    ]
    return lax.ppermute(value, ("az", "ax"), pairs)


def swapped_ax(value, odd):
    count = lax.axis_size("ax")
    pairs = [(q, q + (1 if q % 2 == odd else -1)) for q in range(count)]
    return lax.ppermute(value, "ax", [(q, to) for q, to in pairs if 0 <= to < count])


def by_parity(axis, body, far, near):
    parity = lax.rem(lax.axis_index(axis), 2)

    @pl.when(parity == 0)
    def _():
        body(near, far)

    @pl.when(parity == 1)
    def _():
        body(far, near)


def lanes(shape):
    return lax.broadcasted_iota(jnp.int32, shape, 1)


def rows(shape):
    return lax.broadcasted_iota(jnp.int32, shape, 0)


def radial_next(v):
    tile = 128
    rolled = [pltpu.roll(v[:, at : at + tile], tile - 1, 1) for at in range(0, v.shape[1], tile)]
    last = lanes(rolled[0].shape) == tile - 1
    rolled.append(jnp.zeros_like(rolled[0]))
    return jnp.concatenate(
        [jnp.where(last, later, part) for part, later in zip(rolled, rolled[1:])], axis=1
    )


def radial_prev(v):
    tile = 128
    rolled = [pltpu.roll(v[:, at : at + tile], 1, 1) for at in range(0, v.shape[1], tile)]
    first = lanes(rolled[0].shape) == 0
    rolled.insert(0, jnp.zeros_like(rolled[0]))
    return jnp.concatenate(
        [jnp.where(first, sooner, part) for sooner, part in zip(rolled, rolled[1:])], axis=1
    )


def axial_next(v, row):
    n = v.shape[0]
    return jnp.where(rows(v.shape) == n - 1, row, pltpu.roll(v, n - 1, 0))


def axial_prev(v, row):
    return jnp.where(rows(v.shape) == 0, row, pltpu.roll(v, 1, 0))


def block(k, height):
    return pl.ds(pl.multiple_of(k * height, height), height)


def pack_az(d, height, a, minus, plus):
    minus[block(2 * d, height)] = a[1][0]
    minus[block(2 * d + 1, height)] = a[2][0]
    plus[block(2 * d, height)] = radial_next(a[0][1]) - a[0][1] + a[2][1]
    plus[block(2 * d + 1, height)] = a[0][1] - axial_next(a[0][1], 0.0) - a[1][1]


def pack_ax(d, devs, a, ax_minus, ax_plus):
    top = a[0][0].shape[0] - 1
    for i in range(2):
        ax_minus[pl.ds(i * devs + d, 1)] = a[0][i][0:1]
        ax_minus[pl.ds((2 + i) * devs + d, 1)] = a[2][i][0:1]
        end = a[1][i][top:]
        ax_plus[pl.ds(i * devs + d, 1)] = end - radial_next(end) - a[2][i][top:]
    ax_plus[pl.ds(2 * devs + d, 1)] = a[1][1][top:] - a[1][0][top:] + a[0][0][top:]
    ax_plus[pl.ds(3 * devs + d, 1)] = a[0][1][top:] - a[1][1][top:]


def edge_kernel(
    per, a_hbm, reluct_hbm, lam_hbm, mag_hbm, reg_hbm, slots_hbm,
    ax_near, ax_far, nu_ref, code_ref, offset_ref, static_ref,
    first_ref, last_ref, lam_ref, mag_ref, reg_ref, slots_ref, sems,
):
    devs = a_hbm.shape[0]
    top = nu_ref.shape[2] - 1
    copies = [
        pltpu.make_async_copy(reluct_hbm, nu_ref, sems.at[0]),
        pltpu.make_async_copy(lam_hbm, lam_ref, sems.at[1]),
        pltpu.make_async_copy(mag_hbm, mag_ref, sems.at[2]),
        pltpu.make_async_copy(reg_hbm, reg_ref, sems.at[3]),
        pltpu.make_async_copy(slots_hbm, slots_ref, sems.at[4]),
    ]
    row_copies = []
    for c in range(3):
        for i in range(2):
            to = first_ref.at[pl.ds((2 * c + i) * devs, devs)]
            if c != 1:
                row_copies.append((a_hbm.at[:, c, i, 0], to))
            to = last_ref.at[pl.ds((2 * c + i) * devs, devs)]
            row_copies.append((a_hbm.at[:, c, i, top], to))
    for k, (source, to) in enumerate(row_copies):
        copies.append(pltpu.make_async_copy(source, to, sems.at[5 + k]))
    for copy in copies:
        copy.start()
    for copy in copies[:5]:
        copy.wait()

    base = lax.axis_index("az") * per
    slots = slots_ref[...]
    count = slots.shape[1]
    slots = pltpu.roll(slots, lax.rem(2 * count - base + per, count), 1)
    row = lax.div(slots, jnp.int32(per))
    offset_ref[...] = row * (3 * devs * per) + (slots - row * per)
    for i in range(2):
        nu_ref[1, i] = nu_ref[1, i] * (1.0 + 3.0 * lam_ref[i].astype(jnp.float32))
        code_ref[i] = jnp.where(mag_ref[i] == 1, reg_ref[i] - base, -1).astype(jnp.float32)
    height = top + 1
    static_ref[pl.ds(0, height)] = nu_ref[1, 1]
    static_ref[pl.ds(height, height)] = nu_ref[2, 1]
    static_ref[pl.ds(2 * height, height)] = code_ref[1]
    for copy in copies[5:]:
        copy.wait()

    def body(ax_plus, ax_minus):
        for i in range(2):
            at = 5 * devs + i
            ax_plus[pl.ds(at, 1)] = nu_ref[0, i, top:]
            ax_plus[pl.ds(at + 2, 1)] = nu_ref[2, i, top:]
            ax_plus[pl.ds(at + 4, 1)] = code_ref[i, top:]
            ax_plus[pl.ds(at + 6, 1)] = jnp.zeros_like(code_ref[i, top:])

        firsts = [first_ref[pl.ds(k * devs, devs)] for k in (0, 1, 4, 5)]
        lasts = [[last_ref[pl.ds((2 * c + i) * devs, devs)] for i in range(2)] for c in range(3)]
        for k, first in enumerate(firsts):
            ax_minus[pl.ds(k * devs, devs)] = first
        for i in range(2):
            ax_plus[pl.ds(i * devs, devs)] = lasts[1][i] - radial_next(lasts[1][i]) - lasts[2][i]
        ax_plus[pl.ds(2 * devs, devs)] = lasts[1][1] - lasts[1][0] + lasts[0][0]
        ax_plus[pl.ds(3 * devs, devs)] = lasts[0][1] - lasts[1][1]
        ax_plus[pl.ds(4 * devs, devs)] = lasts[1][0]

    by_parity("ax", body, ax_far, ax_near)


def plane_kernel(a_ref, static_ref, far, near):
    devs, height = a_ref.shape[0], a_ref.shape[3]

    def body(plus, minus):
        plus[pl.ds(2 * devs * height + devs, 3 * height)] = static_ref[...]

        @pl.loop(0, devs, unroll=UNROLL)
        def _(d):
            a = [[a_ref[d, c, i] for i in range(2)] for c in range(3)]
            pack_az(d, height, a, minus, plus)

    by_parity("az", body, far, near)


def corner_kernel(end, devs, ax_near, ax_far, far_in, near_in, far, near, sems):
    at = pl.ds(end, devs)

    def body_ax(ax_ahead, ax_behind):
        def body(plus, minus):
            copies = [
                (ax_behind.at[pl.ds(4 * devs, devs)], minus.at[at]),
                (ax_ahead.at[pl.ds(devs, devs)], plus.at[at]),
            ]
            copies = [
                pltpu.make_async_copy(source, to, sems.at[k]) for k, (source, to) in enumerate(copies)
            ]
            for copy in copies:
                copy.start()
            for copy in copies:
                copy.wait()

        by_parity("az", body, far, near)

    by_parity("ax", body_ax, ax_far, ax_near)


def settle_kernel(halo_near, halo_far, a_ref, ahead, behind, minus):
    devs = a_ref.shape[0]

    def body(ahead_ref, behind_ref):
        ahead[...] = ahead_ref[pl.ds(0, ahead.shape[0])]
        behind[...] = behind_ref[...]

    by_parity("ax", body, halo_far, halo_near)
    for d in range(devs):
        for i in range(2):
            minus[i * devs + d : i * devs + d + 1] = a_ref[d, 0, i, 0:1]
            minus[(2 + i) * devs + d : (2 + i) * devs + d + 1] = a_ref[d, 2, i, 0:1]


def picked(nu, code, values):
    rest, weight = code, 1
    while weight < len(values):
        weight *= 2
    values = list(values) + [values[-1]] * (weight - len(values))
    while len(values) > 1:
        weight //= 2
        high = rest > weight - 0.5
        rest = jnp.where(high, rest - weight, rest)
        half = len(values) // 2
        values = [jnp.where(high, b, a) for a, b in zip(values[:half], values[half:])]
    return jnp.where(code > -0.5, nu * values[0], 0.0)


def advanced(stage, value, start, curl):
    if stage == 0:
        return value * (1.0 - mass_term / cheb_centre) - curl * (1.0 / cheb_centre)
    if stage == 1:
        return (
            value * (1.0 + mix_second - mass_term * step_second) - start * mix_second - curl * step_second
        )
    return -curl - mass_term * value


def flux_of(d, devs, a, up1, up2, ax_ahead):
    flux = [[None, None], [None, None], [None, None]]
    for i in range(2):
        next1 = a[1][1] if i == 0 else up1
        next2 = a[2][1] if i == 0 else up2
        row0 = ax_ahead[pl.ds(i * devs + d, 1)]
        row2 = ax_ahead[pl.ds((2 + i) * devs + d, 1)]
        flux[0][i] = (axial_next(a[2][i], row2) - a[2][i]) - (radial_next(a[1][i]) - a[1][i])
        flux[1][i] = (radial_next(a[0][i]) - a[0][i]) - (next2 - a[2][i])
        flux[2][i] = (next1 - a[1][i]) - (axial_next(a[0][i], row0) - a[0][i])
    return flux


def flux_kernel(a_ref, nu_ref, src_ref, ax_ahead, out_ref):
    devs = a_ref.shape[0]

    @pl.loop(0, devs, unroll=UNROLL)
    def _(d):
        a = [[a_ref[d, c, i] for i in range(2)] for c in range(3)]
        flux = flux_of(d, devs, a, 0.0, 0.0, ax_ahead)
        for c in range(3):
            for i in range(2):
                out_ref[d, c, i] = nu_ref[c, i] * flux[c][i] - src_ref[d, c, i]


def step_kernel(stage, per, *refs):
    refs = list(refs)
    halo = [refs.pop(4), refs.pop(4)]
    statics = refs.pop(2), refs.pop(2)
    sent = [None, None]
    if stage < 2:
        first = (10, 12)[stage]
        sent = [refs.pop(first), refs.pop(first)]

    def body(plus, minus):
        step_body(stage, per, refs, plus, minus)

    by_parity("az", body, (halo[0], statics[0], sent[0]), (halo[1], statics[1], sent[1]))


def step_body(stage, per, refs, beyond_refs, behind_refs):
    it = iter(refs)
    ahead, _, plus = beyond_refs
    behind, nu_az_ref, minus = behind_refs
    a_ref, nu_ref, nu_ax_ref = next(it), next(it), next(it)
    ax_ahead, ax_behind, mine = [next(it) for _ in range(3)]
    if stage == 0:
        code_ref, offset_ref, table_ref = next(it), next(it), next(it)
    else:
        src_ref, src_az_ref, src_ax_ref, track0 = [next(it) for _ in range(4)]
    track = track0 if stage == 1 else None
    if stage == 1:
        start_ref = next(it)
    if stage == 2:
        track = next(it)
    out_ref = next(it)
    if stage < 2:
        ax_minus, ax_plus, next_track = [next(it) for _ in range(3)]
    if stage == 0:
        src_ref, src_az_ref, src_ax_ref = next(it), next(it), next(it)
    if stage == 2:
        final_hbm = next(it)
    edge, corner = next(it), next(it)
    if stage == 2:
        res_hbm, out_ref, sems = out_ref, next(it), next(it)
        leave = pltpu.make_async_copy(a_ref, final_hbm, sems.at[0])
        leave.start()
    devs, height = a_ref.shape[0], a_ref.shape[3]
    top = height - 1
    end = 2 * devs * height
    nu_az = end + devs
    nu_ax = 5 * devs
    every = pl.ds(0, devs)
    after = pl.ds(devs, devs)

    if stage == 0:
        corner[every] = behind[pl.ds(end, devs)]
        corner[after] = ahead[pl.ds(end, devs)]
    else:
        curl = ax_ahead[pl.ds(4 * devs, devs)] - track[pl.ds(2 * devs, devs)]
        value = advanced(stage - 1, track[every], track0[every], curl)
        open_end = lax.axis_index("ax") == lax.axis_size("ax") - 1
        corner[every] = jnp.where(open_end, 0.0, value)
        curl = ahead[pl.ds(end, devs)] + track[pl.ds(3 * devs, devs)]
        corner[after] = advanced(stage - 1, track[after], track0[after], curl)

    def values(d, c, first):
        return [
            table_ref[offset_ref[d, first + k] + (c * devs + d) * per] for k in range(per)
        ]

    if stage == 0:

        @pl.loop(0, devs, unroll=UNROLL)
        def _(d):
            for c in (0, 2):
                own = values(d, c, per)
                for i in range(2):
                    src_ax_ref[pl.ds((c + i) * devs + d, 1)] = picked(
                        nu_ax_ref[pl.ds(nu_ax + c + i, 1)], nu_ax_ref[pl.ds(nu_ax + 4 + i, 1)], own
                    )

    for at, own, sign in ((0, 2, 1.0), (1, 3, 1.0), (2, 0, -1.0), (3, 1, -1.0)):
        part = pl.ds(at * devs, devs)
        flux = ax_behind[part] + sign * mine[pl.ds(own * devs, devs)]
        if at == 3:
            flux = flux + corner[after]
        edge[part] = nu_ax_ref[pl.ds(nu_ax + at, 1)] * flux - src_ax_ref[part]
    if stage < 2:
        before = edge[every]
        minus[pl.ds(end, devs)] = before - radial_prev(before) - edge[pl.ds(2 * devs, devs)]
        next_track[pl.ds(0, 2 * devs)] = corner[...]
        next_track[pl.ds(3 * devs, devs)] = edge[pl.ds(3 * devs, devs)]

    @pl.loop(0, devs, unroll=UNROLL)
    def _(d):
        a = [[a_ref[d, c, i] for i in range(2)] for c in range(3)]
        up = [None, ahead[block(2 * d, height)], ahead[block(2 * d + 1, height)]]
        inten = [[None, None], [None, None], [None, None]]
        own = [values(d, c, per) for c in range(3)] if stage == 0 else None
        if stage == 0:
            fluxes = flux_of(d, devs, a, up[1], up[2], ax_ahead)
        for i in range(2):
            for c in range(3):
                if stage == 0:
                    src = picked(nu_ref[c, i], code_ref[i], own[c])
                    src_ref[d, c, i] = src
                    inten[c][i] = nu_ref[c, i] * fluxes[c][i] - src
                else:
                    inten[c][i] = src_ref[d, c, i]
        if stage > 0:
            inten[1][1] = inten[1][1] - nu_ref[1, 1] * up[2]
            inten[2][1] = inten[2][1] + nu_ref[2, 1] * up[1]
        back_src = [None, None]
        for c in range(1, 3):
            if stage == 0:
                src = picked(
                    nu_az_ref[pl.ds(nu_az + (c - 1) * height, height)],
                    nu_az_ref[pl.ds(nu_az + 2 * height, height)],
                    values(d, c, 0),
                )
                src_az_ref[2 * d + c - 1] = src
            else:
                src = src_az_ref[2 * d + c - 1]
            back_src[c - 1] = src
        beyond = jnp.where(rows(a[1][0].shape) == top, corner[pl.ds(d, 1)], 0.0)
        back1 = nu_az_ref[pl.ds(nu_az, height)] * (behind[block(2 * d, height)] - a[2][0]) - back_src[0]
        back2 = (
            nu_az_ref[pl.ds(nu_az + height, height)]
            * (behind[block(2 * d + 1, height)] + a[1][0] - beyond)
            - back_src[1]
        )
        new = [[None, None], [None, None], [None, None]]
        for i in range(2):
            prev1 = back1 if i == 0 else inten[1][0]
            prev2 = back2 if i == 0 else inten[2][0]
            row0 = edge[pl.ds(i * devs + d, 1)]
            row2 = edge[pl.ds((2 + i) * devs + d, 1)]
            i0, i1, i2 = inten[0][i], inten[1][i], inten[2][i]
            curl = (
                (i2 - axial_prev(i2, row2)) - (i1 - radial_prev(i1)),
                (i0 - radial_prev(i0)) - (i2 - prev2),
                (i1 - prev1) - (i0 - axial_prev(i0, row0)),
            )
            for c in range(3):
                start = start_ref[d, c, i] if stage == 1 else None
                value = advanced(stage, a[c][i], start, curl[c])
                out_ref[d, c, i] = value
                new[c][i] = value
        if stage == 2:
            pltpu.make_async_copy(out_ref.at[d], res_hbm.at[d], sems.at[1]).start()
        if stage < 2:
            first1, first2 = back1[0:1], back2[0:1]
            ax_minus[pl.ds(4 * devs + d, 1)] = first2 - (first1 - radial_prev(first1))
            next_track[pl.ds(2 * devs + d, 1)] = back2[top:]
            pack_az(d, height, new, minus, plus)
            pack_ax(d, devs, new, ax_minus, ax_plus)

    if stage == 2:
        leave.wait()
        pltpu.make_async_copy(out_ref, res_hbm, sems.at[1]).wait()


def f32(*shape):
    return jax.ShapeDtypeStruct(shape, jnp.float32)


def shards(start_field, reluctivity, lamination, magnets, region_ids, pieces, slot_map):
    devs, comps, cells_az, cells_ax, radial = start_field.shape
    count_az = lax.axis_size("az")
    per = pieces.shape[2]
    whole = 2 * devs * cells_ax

    field_like = f32(*start_field.shape)
    edges = [
        f32(5 * devs + 8, radial),
        f32(5 * devs + 8, radial),
        f32(*reluctivity.shape),
        f32(*lamination.shape),
        jax.ShapeDtypeStruct(slot_map.shape, jnp.int32),
        f32(3 * cells_ax, radial),
    ]
    ax_near, ax_far, nu, code, offset, static = pl.pallas_call(
        functools.partial(edge_kernel, per),
        out_shape=edges,
        in_specs=[HBM] * 6,
        out_specs=[VMEM] * len(edges),
        scratch_shapes=[pltpu.VMEM((6 * devs, radial), jnp.float32)] * 2
        + [pltpu.VMEM(lamination.shape, jnp.int32)] * 3
        + [pltpu.VMEM(slot_map.shape, jnp.int32), pltpu.SemaphoreType.DMA((15,))],
        compiler_params=pltpu.CompilerParams(vmem_limit_bytes=LIMIT_FIRST),
    )(start_field, reluctivity, lamination, magnets, region_ids, slot_map)
    ax_halos = swapped_ax(ax_near, 0), swapped_ax(ax_far, 1)
    planes = [f32(whole + devs + 3 * cells_ax, radial)] * 2
    packed = pl.pallas_call(
        plane_kernel,
        out_shape=planes,
        in_specs=[VMEM] * 2,
        out_specs=[VMEM] * 2,
        compiler_params=pltpu.CompilerParams(vmem_limit_bytes=LIMIT),
        cost_estimate=pl.CostEstimate(flops=10**7, bytes_accessed=3 * MIB, transcendentals=0),
    )(start_field, static)
    far, near = pl.pallas_call(
        functools.partial(corner_kernel, whole, devs),
        out_shape=planes,
        in_specs=[VMEM, VMEM, ANY, ANY],
        out_specs=[ANY] * 2,
        scratch_shapes=[pltpu.SemaphoreType.DMA((2,))],
        input_output_aliases={2: 0, 3: 1},
        compiler_params=pltpu.CompilerParams(vmem_limit_bytes=LIMIT),
    )(*ax_halos, *packed)
    ax_ahead, ax_behind, ax_minus = pl.pallas_call(
        settle_kernel,
        out_shape=[f32(4 * devs, radial), f32(5 * devs + 8, radial), f32(4 * devs, radial)],
        in_specs=[VMEM] * 3,
        out_specs=[VMEM] * 3,
        compiler_params=pltpu.CompilerParams(vmem_limit_bytes=LIMIT),
    )(*ax_halos, start_field)
    far_halo, near_halo = swapped(far, 1), swapped(near, 0)
    halos = (far_halo, near_halo, ax_ahead, ax_behind, ax_minus)
    flat = pieces.reshape(1, comps * devs * per)
    table = lax.all_to_all(
        jnp.broadcast_to(flat, (count_az, comps * devs * per)), "az", 0, 0, tiled=True
    ).reshape(-1)

    def exchange(far, near, ax_minus, ax_plus):
        from_far, from_near = swapped(far, 1), swapped(near, 0)
        return from_far, from_near, moved(ax_minus, 0, -1), moved(ax_plus, 0, 1), ax_minus

    def step(stage, field, halos, more, more_specs):
        outs = [field_like]
        if stage < 2:
            outs += [
                f32(whole + devs, radial),
                f32(whole + devs, radial),
                f32(5 * devs, radial),
                f32(4 * devs, radial),
                f32(4 * devs, radial),
            ]
        else:
            outs += [field_like]
        if stage == 0:
            outs += [field_like, f32(2 * devs, cells_ax, radial), f32(4 * devs, radial)]
        return pl.pallas_call(
            functools.partial(step_kernel, stage, per),
            out_shape=outs,
            in_specs=[VMEM] * 10 + more_specs,
            out_specs=[VMEM if stage < 2 else HBM] * len(outs),
            scratch_shapes=[
                pltpu.VMEM((4 * devs, radial), jnp.float32),
                pltpu.VMEM((2 * devs, radial), jnp.float32),
            ]
            + [pltpu.VMEM(start_field.shape, jnp.float32), pltpu.SemaphoreType.DMA((2,))] * (stage // 2),
            compiler_params=pltpu.CompilerParams(vmem_limit_bytes=LIMIT),
        )(field, nu, far_halo, near_halo, *halos[:2], ax_behind, *halos[2:], *more)

    def known(field, halos):
        return pl.pallas_call(
            flux_kernel,
            out_shape=field_like,
            in_specs=[VMEM] * 4,
            out_specs=VMEM,
            compiler_params=pltpu.CompilerParams(vmem_limit_bytes=LIMIT),
            cost_estimate=pl.CostEstimate(flops=10**7, bytes_accessed=5 * MIB, transcendentals=0),
        )(field, nu, src[0], halos[2])

    middle, *rest = step(0, start_field, halos, [code, offset, table], [VMEM, SMEM, SMEM])
    packed, track0, src = rest[:4], rest[4], rest[5:]
    halos = exchange(*packed)
    more = [known(middle, halos), *src[1:], track0, start_field]
    final, *rest = step(1, middle, halos, more, [VMEM] * 5)
    packed, track1 = rest[:4], rest[4]
    halos = exchange(*packed)
    more = [known(final, halos), *src[1:], track0, track1]
    residual, out = step(2, final, halos, more, [VMEM] * 5)
    return out, residual


def solution(mesh):
    placed = (
        P(None, None, "az", "ax", None),
        P(None, "az", "ax", None),
        P("az", "ax", None),
        P("az", "ax", None),
        P("az", "ax", None),
        P(None, None, "az"),
        P(),
    )
    return jax.shard_map(
        shards,
        mesh=mesh,
        in_specs=placed,
        out_specs=(P(None, None, "az", "ax", None), P(None, None, "az", "ax", None)),
        check_vma=False,
    )
```

```python
import functools

import jax
import jax.numpy as jnp
from jax import lax
from jax.experimental import pallas as pl
from jax.experimental.pallas import tpu as pltpu
from jax.sharding import PartitionSpec as P

mass_term = 1.0
cheb_centre = 8.5
cheb_halfwidth = 7.5
cheb_sigma = cheb_centre / cheb_halfwidth
rho_first = 1.0 / cheb_sigma
rho_second = 1.0 / (2.0 * cheb_sigma - rho_first)

mix_second = rho_second * rho_first
step_second = 2.0 * rho_second / cheb_halfwidth

VMEM = pl.BlockSpec(memory_space=pltpu.VMEM)
SMEM = pl.BlockSpec(memory_space=pltpu.SMEM)
HBM = pl.BlockSpec(memory_space=pltpu.HBM)
ANY = pl.BlockSpec(memory_space=pl.ANY)
MIB = 1024 * 1024
LIMIT = 16 * MIB
UNROLL = 4
LIMIT_FIRST = 63 * MIB


def moved(value, shift_az, shift_ax):
    count_az, count_ax = lax.axis_size("az"), lax.axis_size("ax")
    pairs = [
        (a * count_ax + q, (a + shift_az) % count_az * count_ax + q + shift_ax)
        for a in range(count_az)
        for q in range(count_ax)
        if 0 <= q + shift_ax < count_ax
    ]
    return lax.ppermute(value, ("az", "ax"), pairs)


def swapped(value, odd):
    count_az, count_ax = lax.axis_size("az"), lax.axis_size("ax")
    pairs = [
        (a * count_ax + q, (a + (1 if a % 2 == odd else -1)) % count_az * count_ax + q)
        for a in range(count_az)
        for q in range(count_ax)
    ]
    return lax.ppermute(value, ("az", "ax"), pairs)


def swapped_ax(value, odd):
    count = lax.axis_size("ax")
    pairs = [(q, q + (1 if q % 2 == odd else -1)) for q in range(count)]
    return lax.ppermute(value, "ax", [(q, to) for q, to in pairs if 0 <= to < count])


def by_parity(axis, body, far, near):
    parity = lax.rem(lax.axis_index(axis), 2)

    @pl.when(parity == 0)
    def _():
        body(near, far)

    @pl.when(parity == 1)
    def _():
        body(far, near)


def lanes(shape):
    return lax.broadcasted_iota(jnp.int32, shape, 1)


def rows(shape):
    return lax.broadcasted_iota(jnp.int32, shape, 0)


def radial_next(v):
    tile = 128
    rolled = [pltpu.roll(v[:, at : at + tile], tile - 1, 1) for at in range(0, v.shape[1], tile)]
    last = lanes(rolled[0].shape) == tile - 1
    rolled.append(jnp.zeros_like(rolled[0]))
    return jnp.concatenate(
        [jnp.where(last, later, part) for part, later in zip(rolled, rolled[1:])], axis=1
    )


def radial_prev(v):
    tile = 128
    rolled = [pltpu.roll(v[:, at : at + tile], 1, 1) for at in range(0, v.shape[1], tile)]
    first = lanes(rolled[0].shape) == 0
    rolled.insert(0, jnp.zeros_like(rolled[0]))
    return jnp.concatenate(
        [jnp.where(first, sooner, part) for sooner, part in zip(rolled, rolled[1:])], axis=1
    )


def axial_next(v, row):
    n = v.shape[0]
    return jnp.where(rows(v.shape) == n - 1, row, pltpu.roll(v, n - 1, 0))


def axial_prev(v, row):
    return jnp.where(rows(v.shape) == 0, row, pltpu.roll(v, 1, 0))


def block(k, height):
    return pl.ds(pl.multiple_of(k * height, height), height)


def pack_az(d, height, a, minus, plus):
    minus[block(2 * d, height)] = a[1][0]
    minus[block(2 * d + 1, height)] = a[2][0]
    plus[block(2 * d, height)] = radial_next(a[0][1]) - a[0][1] + a[2][1]
    plus[block(2 * d + 1, height)] = a[0][1] - axial_next(a[0][1], 0.0) - a[1][1]


def pack_ax(d, devs, a, ax_minus, ax_plus):
    top = a[0][0].shape[0] - 1
    for i in range(2):
        ax_minus[pl.ds(i * devs + d, 1)] = a[0][i][0:1]
        ax_minus[pl.ds((2 + i) * devs + d, 1)] = a[2][i][0:1]
        end = a[1][i][top:]
        ax_plus[pl.ds(i * devs + d, 1)] = end - radial_next(end) - a[2][i][top:]
    ax_plus[pl.ds(2 * devs + d, 1)] = a[1][1][top:] - a[1][0][top:] + a[0][0][top:]
    ax_plus[pl.ds(3 * devs + d, 1)] = a[0][1][top:] - a[1][1][top:]


def edge_kernel(
    per, a_hbm, reluct_hbm, lam_hbm, mag_hbm, reg_hbm, slots_hbm,
    ax_near, ax_far, nu_ref, code_ref, offset_ref, static_ref,
    first_ref, last_ref, lam_ref, mag_ref, reg_ref, slots_ref, sems,
):
    devs = a_hbm.shape[0]
    top = nu_ref.shape[2] - 1
    copies = [
        pltpu.make_async_copy(reluct_hbm, nu_ref, sems.at[0]),
        pltpu.make_async_copy(lam_hbm, lam_ref, sems.at[1]),
        pltpu.make_async_copy(mag_hbm, mag_ref, sems.at[2]),
        pltpu.make_async_copy(reg_hbm, reg_ref, sems.at[3]),
        pltpu.make_async_copy(slots_hbm, slots_ref, sems.at[4]),
    ]
    row_copies = []
    for c in range(3):
        for i in range(2):
            to = first_ref.at[pl.ds((2 * c + i) * devs, devs)]
            if c != 1:
                row_copies.append((a_hbm.at[:, c, i, 0], to))
            to = last_ref.at[pl.ds((2 * c + i) * devs, devs)]
            row_copies.append((a_hbm.at[:, c, i, top], to))
    for k, (source, to) in enumerate(row_copies):
        copies.append(pltpu.make_async_copy(source, to, sems.at[5 + k]))
    for copy in copies:
        copy.start()
    for copy in copies[:5]:
        copy.wait()

    base = lax.axis_index("az") * per
    slots = slots_ref[...]
    count = slots.shape[1]
    slots = pltpu.roll(slots, lax.rem(2 * count - base + per, count), 1)
    row = lax.div(slots, jnp.int32(per))
    offset_ref[...] = row * (3 * devs * per) + (slots - row * per)
    for i in range(2):
        nu_ref[1, i] = nu_ref[1, i] * (1.0 + 3.0 * lam_ref[i].astype(jnp.float32))
        code_ref[i] = jnp.where(mag_ref[i] == 1, reg_ref[i] - base, -1).astype(jnp.float32)
    height = top + 1
    static_ref[pl.ds(0, height)] = nu_ref[1, 1]
    static_ref[pl.ds(height, height)] = nu_ref[2, 1]
    static_ref[pl.ds(2 * height, height)] = code_ref[1]
    for copy in copies[5:]:
        copy.wait()

    def body(ax_plus, ax_minus):
        for i in range(2):
            at = 5 * devs + i
            ax_plus[pl.ds(at, 1)] = nu_ref[0, i, top:]
            ax_plus[pl.ds(at + 2, 1)] = nu_ref[2, i, top:]
            ax_plus[pl.ds(at + 4, 1)] = code_ref[i, top:]
            ax_plus[pl.ds(at + 6, 1)] = code_ref[i, top:]

        firsts = [first_ref[pl.ds(k * devs, devs)] for k in (0, 1, 4, 5)]
        lasts = [[last_ref[pl.ds((2 * c + i) * devs, devs)] for i in range(2)] for c in range(3)]
        for k, first in enumerate(firsts):
            ax_minus[pl.ds(k * devs, devs)] = first
        for i in range(2):
            ax_plus[pl.ds(i * devs, devs)] = lasts[1][i] - radial_next(lasts[1][i]) - lasts[2][i]
        ax_plus[pl.ds(2 * devs, devs)] = lasts[1][1] - lasts[1][0] + lasts[0][0]
        ax_plus[pl.ds(3 * devs, devs)] = lasts[0][1] - lasts[1][1]
        ax_plus[pl.ds(4 * devs, devs)] = lasts[1][0]

    by_parity("ax", body, ax_far, ax_near)


def plane_kernel(a_ref, static_ref, far, near):
    devs, height = a_ref.shape[0], a_ref.shape[3]

    def body(plus, minus):
        plus[pl.ds(2 * devs * height + devs, 3 * height)] = static_ref[...]

        @pl.loop(0, devs, unroll=UNROLL)
        def _(d):
            a = [[a_ref[d, c, i] for i in range(2)] for c in range(3)]
            pack_az(d, height, a, minus, plus)

    by_parity("az", body, far, near)


def corner_kernel(end, devs, ax_near, ax_far, far_in, near_in, far, near, sems):
    at = pl.ds(end, devs)

    def body_ax(ax_ahead, ax_behind):
        def body(plus, minus):
            copies = [
                (ax_behind.at[pl.ds(4 * devs, devs)], minus.at[at]),
                (ax_ahead.at[pl.ds(devs, devs)], plus.at[at]),
            ]
            copies = [
                pltpu.make_async_copy(source, to, sems.at[k]) for k, (source, to) in enumerate(copies)
            ]
            for copy in copies:
                copy.start()
            for copy in copies:
                copy.wait()

        by_parity("az", body, far, near)

    by_parity("ax", body_ax, ax_far, ax_near)


def settle_kernel(halo_near, halo_far, a_ref, ahead, behind, minus):
    devs = a_ref.shape[0]

    def body(ahead_ref, behind_ref):
        ahead[...] = ahead_ref[pl.ds(0, ahead.shape[0])]
        behind[...] = behind_ref[...]

    by_parity("ax", body, halo_far, halo_near)
    for d in range(devs):
        for i in range(2):
            minus[i * devs + d : i * devs + d + 1] = a_ref[d, 0, i, 0:1]
            minus[(2 + i) * devs + d : (2 + i) * devs + d + 1] = a_ref[d, 2, i, 0:1]


def picked(nu, code, values):
    rest, weight = code, 1
    while weight < len(values):
        weight *= 2
    values = list(values) + [values[-1]] * (weight - len(values))
    while len(values) > 1:
        weight //= 2
        high = rest > weight - 0.5
        rest = jnp.where(high, rest - weight, rest)
        half = len(values) // 2
        values = [jnp.where(high, b, a) for a, b in zip(values[:half], values[half:])]
    return jnp.where(code > -0.5, nu * values[0], 0.0)


def advanced(stage, value, start, curl):
    if stage == 0:
        return value * (1.0 - mass_term / cheb_centre) - curl * (1.0 / cheb_centre)
    if stage == 1:
        return (
            value * (1.0 + mix_second - mass_term * step_second) - start * mix_second - curl * step_second
        )
    return -curl - mass_term * value


def flux_of(d, devs, a, up1, up2, ax_ahead):
    flux = [[None, None], [None, None], [None, None]]
    for i in range(2):
        next1 = a[1][1] if i == 0 else up1
        next2 = a[2][1] if i == 0 else up2
        row0 = ax_ahead[pl.ds(i * devs + d, 1)]
        row2 = ax_ahead[pl.ds((2 + i) * devs + d, 1)]
        flux[0][i] = (axial_next(a[2][i], row2) - a[2][i]) - (radial_next(a[1][i]) - a[1][i])
        flux[1][i] = (radial_next(a[0][i]) - a[0][i]) - (next2 - a[2][i])
        flux[2][i] = (next1 - a[1][i]) - (axial_next(a[0][i], row0) - a[0][i])
    return flux


def flux_kernel(a_ref, nu_ref, src_ref, ax_ahead, out_ref):
    devs = a_ref.shape[0]

    @pl.loop(0, devs, unroll=UNROLL)
    def _(d):
        a = [[a_ref[d, c, i] for i in range(2)] for c in range(3)]
        flux = flux_of(d, devs, a, 0.0, 0.0, ax_ahead)
        for c in range(3):
            for i in range(2):
                out_ref[d, c, i] = nu_ref[c, i] * flux[c][i] - src_ref[d, c, i]


def step_kernel(stage, per, *refs):
    refs = list(refs)
    halo = [refs.pop(4), refs.pop(4)]
    statics = refs.pop(2), refs.pop(2)
    sent = [None, None]
    if stage < 2:
        first = (10, 12)[stage]
        sent = [refs.pop(first), refs.pop(first)]

    def body(plus, minus):
        step_body(stage, per, refs, plus, minus)

    by_parity("az", body, (halo[0], statics[0], sent[0]), (halo[1], statics[1], sent[1]))


def step_body(stage, per, refs, beyond_refs, behind_refs):
    it = iter(refs)
    ahead, _, plus = beyond_refs
    behind, nu_az_ref, minus = behind_refs
    a_ref, nu_ref, nu_ax_ref = next(it), next(it), next(it)
    ax_ahead, ax_behind, mine = [next(it) for _ in range(3)]
    if stage == 0:
        code_ref, offset_ref, table_ref = next(it), next(it), next(it)
    else:
        src_ref, src_az_ref, src_ax_ref, track0 = [next(it) for _ in range(4)]
    track = track0 if stage == 1 else None
    if stage == 1:
        start_ref = next(it)
    if stage == 2:
        track = next(it)
    out_ref = next(it)
    if stage < 2:
        ax_minus, ax_plus, next_track = [next(it) for _ in range(3)]
    if stage == 0:
        src_ref, src_az_ref, src_ax_ref = next(it), next(it), next(it)
    if stage == 2:
        final_hbm = next(it)
    edge, corner = next(it), next(it)
    if stage == 2:
        res_hbm, out_ref, sems = out_ref, next(it), next(it)
        leave = pltpu.make_async_copy(a_ref, final_hbm, sems.at[0])
        leave.start()
    devs, height = a_ref.shape[0], a_ref.shape[3]
    top = height - 1
    end = 2 * devs * height
    nu_az = end + devs
    nu_ax = 5 * devs
    every = pl.ds(0, devs)
    after = pl.ds(devs, devs)

    if stage == 0:
        corner[every] = behind[pl.ds(end, devs)]
        corner[after] = ahead[pl.ds(end, devs)]
    else:
        curl = ax_ahead[pl.ds(4 * devs, devs)] - track[pl.ds(2 * devs, devs)]
        value = advanced(stage - 1, track[every], track0[every], curl)
        open_end = lax.axis_index("ax") == lax.axis_size("ax") - 1
        corner[every] = jnp.where(open_end, 0.0, value)
        curl = ahead[pl.ds(end, devs)] + track[pl.ds(3 * devs, devs)]
        corner[after] = advanced(stage - 1, track[after], track0[after], curl)

    def values(d, c, first):
        return [
            table_ref[offset_ref[d, first + k] + (c * devs + d) * per] for k in range(per)
        ]

    if stage == 0:
        nu_rows = nu_ax_ref[pl.ds(nu_ax, 4)]
        code_rows = nu_ax_ref[pl.ds(nu_ax + 4, 4)]
        upper = rows(nu_rows.shape) < 2

        @pl.loop(0, devs, unroll=UNROLL)
        def _(d):
            both = [jnp.where(upper, x, y) for x, y in zip(values(d, 0, per), values(d, 2, per))]
            four = picked(nu_rows, code_rows, both)
            for k in range(4):
                src_ax_ref[pl.ds(k * devs + d, 1)] = four[k : k + 1]

    for at, own, sign in ((0, 2, 1.0), (1, 3, 1.0), (2, 0, -1.0), (3, 1, -1.0)):
        part = pl.ds(at * devs, devs)
        flux = ax_behind[part] + sign * mine[pl.ds(own * devs, devs)]
        if at == 3:
            flux = flux + corner[after]
        edge[part] = nu_ax_ref[pl.ds(nu_ax + at, 1)] * flux - src_ax_ref[part]
    if stage < 2:
        before = edge[every]
        minus[pl.ds(end, devs)] = before - radial_prev(before) - edge[pl.ds(2 * devs, devs)]
        next_track[pl.ds(0, 2 * devs)] = corner[...]
        next_track[pl.ds(3 * devs, devs)] = edge[pl.ds(3 * devs, devs)]

    @pl.loop(0, devs, unroll=UNROLL)
    def _(d):
        a = [[a_ref[d, c, i] for i in range(2)] for c in range(3)]
        up = [None, ahead[block(2 * d, height)], ahead[block(2 * d + 1, height)]]
        inten = [[None, None], [None, None], [None, None]]
        own = [values(d, c, per) for c in range(3)] if stage == 0 else None
        if stage == 0:
            fluxes = flux_of(d, devs, a, up[1], up[2], ax_ahead)
        for i in range(2):
            for c in range(3):
                if stage == 0:
                    src = picked(nu_ref[c, i], code_ref[i], own[c])
                    src_ref[d, c, i] = src
                    inten[c][i] = nu_ref[c, i] * fluxes[c][i] - src
                else:
                    inten[c][i] = src_ref[d, c, i]
        if stage > 0:
            inten[1][1] = inten[1][1] - nu_ref[1, 1] * up[2]
            inten[2][1] = inten[2][1] + nu_ref[2, 1] * up[1]
        back_src = [None, None]
        for c in range(1, 3):
            if stage == 0:
                src = picked(
                    nu_az_ref[pl.ds(nu_az + (c - 1) * height, height)],
                    nu_az_ref[pl.ds(nu_az + 2 * height, height)],
                    values(d, c, 0),
                )
                src_az_ref[2 * d + c - 1] = src
            else:
                src = src_az_ref[2 * d + c - 1]
            back_src[c - 1] = src
        beyond = jnp.where(rows(a[1][0].shape) == top, corner[pl.ds(d, 1)], 0.0)
        back1 = nu_az_ref[pl.ds(nu_az, height)] * (behind[block(2 * d, height)] - a[2][0]) - back_src[0]
        back2 = (
            nu_az_ref[pl.ds(nu_az + height, height)]
            * (behind[block(2 * d + 1, height)] + a[1][0] - beyond)
            - back_src[1]
        )
        new = [[None, None], [None, None], [None, None]]
        for i in range(2):
            prev1 = back1 if i == 0 else inten[1][0]
            prev2 = back2 if i == 0 else inten[2][0]
            row0 = edge[pl.ds(i * devs + d, 1)]
            row2 = edge[pl.ds((2 + i) * devs + d, 1)]
            i0, i1, i2 = inten[0][i], inten[1][i], inten[2][i]
            curl = (
                (i2 - axial_prev(i2, row2)) - (i1 - radial_prev(i1)),
                (i0 - radial_prev(i0)) - (i2 - prev2),
                (i1 - prev1) - (i0 - axial_prev(i0, row0)),
            )
            for c in range(3):
                start = start_ref[d, c, i] if stage == 1 else None
                value = advanced(stage, a[c][i], start, curl[c])
                out_ref[d, c, i] = value
                new[c][i] = value
        if stage == 2:
            pltpu.make_async_copy(out_ref.at[d], res_hbm.at[d], sems.at[1]).start()
        if stage < 2:
            first1, first2 = back1[0:1], back2[0:1]
            ax_minus[pl.ds(4 * devs + d, 1)] = first2 - (first1 - radial_prev(first1))
            next_track[pl.ds(2 * devs + d, 1)] = back2[top:]
            pack_az(d, height, new, minus, plus)
            pack_ax(d, devs, new, ax_minus, ax_plus)

    if stage == 2:
        leave.wait()
        pltpu.make_async_copy(out_ref, res_hbm, sems.at[1]).wait()


def f32(*shape):
    return jax.ShapeDtypeStruct(shape, jnp.float32)


def shards(start_field, reluctivity, lamination, magnets, region_ids, pieces, slot_map):
    devs, comps, cells_az, cells_ax, radial = start_field.shape
    count_az = lax.axis_size("az")
    per = pieces.shape[2]
    whole = 2 * devs * cells_ax

    field_like = f32(*start_field.shape)
    edges = [
        f32(5 * devs + 8, radial),
        f32(5 * devs + 8, radial),
        f32(*reluctivity.shape),
        f32(*lamination.shape),
        jax.ShapeDtypeStruct(slot_map.shape, jnp.int32),
        f32(3 * cells_ax, radial),
    ]
    ax_near, ax_far, nu, code, offset, static = pl.pallas_call(
        functools.partial(edge_kernel, per),
        out_shape=edges,
        in_specs=[HBM] * 6,
        out_specs=[VMEM] * len(edges),
        scratch_shapes=[pltpu.VMEM((6 * devs, radial), jnp.float32)] * 2
        + [pltpu.VMEM(lamination.shape, jnp.int32)] * 3
        + [pltpu.VMEM(slot_map.shape, jnp.int32), pltpu.SemaphoreType.DMA((15,))],
        compiler_params=pltpu.CompilerParams(vmem_limit_bytes=LIMIT_FIRST),
    )(start_field, reluctivity, lamination, magnets, region_ids, slot_map)
    ax_halos = swapped_ax(ax_near, 0), swapped_ax(ax_far, 1)
    planes = [f32(whole + devs + 3 * cells_ax, radial)] * 2
    packed = pl.pallas_call(
        plane_kernel,
        out_shape=planes,
        in_specs=[VMEM] * 2,
        out_specs=[VMEM] * 2,
        compiler_params=pltpu.CompilerParams(vmem_limit_bytes=LIMIT),
        cost_estimate=pl.CostEstimate(flops=10**7, bytes_accessed=3 * MIB, transcendentals=0),
    )(start_field, static)
    far, near = pl.pallas_call(
        functools.partial(corner_kernel, whole, devs),
        out_shape=planes,
        in_specs=[VMEM, VMEM, ANY, ANY],
        out_specs=[ANY] * 2,
        scratch_shapes=[pltpu.SemaphoreType.DMA((2,))],
        input_output_aliases={2: 0, 3: 1},
        compiler_params=pltpu.CompilerParams(vmem_limit_bytes=LIMIT),
    )(*ax_halos, *packed)
    ax_ahead, ax_behind, ax_minus = pl.pallas_call(
        settle_kernel,
        out_shape=[f32(4 * devs, radial), f32(5 * devs + 8, radial), f32(4 * devs, radial)],
        in_specs=[VMEM] * 3,
        out_specs=[VMEM] * 3,
        compiler_params=pltpu.CompilerParams(vmem_limit_bytes=LIMIT),
    )(*ax_halos, start_field)
    far_halo, near_halo = swapped(far, 1), swapped(near, 0)
    halos = (far_halo, near_halo, ax_ahead, ax_behind, ax_minus)
    flat = pieces.reshape(1, comps * devs * per)
    table = lax.all_to_all(
        jnp.broadcast_to(flat, (count_az, comps * devs * per)), "az", 0, 0, tiled=True
    ).reshape(-1)

    def exchange(far, near, ax_minus, ax_plus):
        from_far, from_near = swapped(far, 1), swapped(near, 0)
        return from_far, from_near, moved(ax_minus, 0, -1), moved(ax_plus, 0, 1), ax_minus

    def step(stage, field, halos, more, more_specs):
        outs = [field_like]
        if stage < 2:
            outs += [
                f32(whole + devs, radial),
                f32(whole + devs, radial),
                f32(5 * devs, radial),
                f32(4 * devs, radial),
                f32(4 * devs, radial),
            ]
        else:
            outs += [field_like]
        if stage == 0:
            outs += [field_like, f32(2 * devs, cells_ax, radial), f32(4 * devs, radial)]
        return pl.pallas_call(
            functools.partial(step_kernel, stage, per),
            out_shape=outs,
            in_specs=[VMEM] * 10 + more_specs,
            out_specs=[VMEM if stage < 2 else HBM] * len(outs),
            scratch_shapes=[
                pltpu.VMEM((4 * devs, radial), jnp.float32),
                pltpu.VMEM((2 * devs, radial), jnp.float32),
            ]
            + [pltpu.VMEM(start_field.shape, jnp.float32), pltpu.SemaphoreType.DMA((2,))] * (stage // 2),
            compiler_params=pltpu.CompilerParams(vmem_limit_bytes=LIMIT),
        )(field, nu, far_halo, near_halo, *halos[:2], ax_behind, *halos[2:], *more)

    def known(field, halos):
        return pl.pallas_call(
            flux_kernel,
            out_shape=field_like,
            in_specs=[VMEM] * 4,
            out_specs=VMEM,
            compiler_params=pltpu.CompilerParams(vmem_limit_bytes=LIMIT),
            cost_estimate=pl.CostEstimate(flops=10**7, bytes_accessed=5 * MIB, transcendentals=0),
        )(field, nu, src[0], halos[2])

    middle, *rest = step(0, start_field, halos, [code, offset, table], [VMEM, SMEM, SMEM])
    packed, track0, src = rest[:4], rest[4], rest[5:]
    halos = exchange(*packed)
    more = [known(middle, halos), *src[1:], track0, start_field]
    final, *rest = step(1, middle, halos, more, [VMEM] * 5)
    packed, track1 = rest[:4], rest[4]
    halos = exchange(*packed)
    more = [known(final, halos), *src[1:], track0, track1]
    residual, out = step(2, final, halos, more, [VMEM] * 5)
    return out, residual


def solution(mesh):
    placed = (
        P(None, None, "az", "ax", None),
        P(None, "az", "ax", None),
        P("az", "ax", None),
        P("az", "ax", None),
        P("az", "ax", None),
        P(None, None, "az"),
        P(),
    )
    return jax.shard_map(
        shards,
        mesh=mesh,
        in_specs=placed,
        out_specs=(P(None, None, "az", "ax", None), P(None, None, "az", "ax", None)),
        check_vma=False,
    )
```
